32 devices in a mesh: req: 2 (over y), seq: 4 (over z), branch: 2 (over core), tp: 2 (over x).
Axes of the slice: x: 2, y: 2, z: 4, core: 2. Of those that a mesh axis runs over, the one named last changes fastest.
Arguments:
- projected: bfloat16 [2, 768, 3, 4096], P('branch', ('req', 'seq', 'tp')), parts along dimension 1, may hold values from -24 to 24
- hint_gain: float32 [4096], replicated, may hold values from 0.3 to 1.5
- block_map: int32 [4], replicated, may hold values from 0 to 3, each once
- token_perm: int32 [8, 48], replicated, may hold values from 0 to 47, each once within a row
Outputs:
- combined: bfloat16 [2, 768, 4096], P('branch', ('req', 'seq', 'tp')), parts along dimension 1
The draws below stay inside these ranges and needn't reach their ends.
There are 2 independent parts, one for each index of `req`. The reference program is written for one: setup_inputs(seed, part) draws one part's arguments, and reference() takes and returns one part's arrays. A program takes and returns all parts, laid end to end along the dimension named above; an argument that names none is the same for every part. Nothing has to cross between parts.
Inputs may be any that keep to these rules, and one draw needn't show every extreme that they name: `block_map`: a permutation of the 4 sequence shards. `token_perm`: each row is a permutation of 0 to 47.
All inputs are finite; a program needn't handle non-finite values.
Results may differ from the reference program's by a relative error of at most 0.0055.
Values may be sent and summed in bfloat16 or wider, within the bound.
No kernel may reach another device: no remote copies, remote signals or barrier semaphores. Data moves between devices by JAX's collectives and lax.ppermute only.
A program may use at most 64 MiB of HBM per device.

```python
import math
import jax
import jax.numpy as jnp
from jax import lax

HD = 128
H = 32
TOK_DEV = 48
TOKENS = 384
ROW = 96
F = 4096
N_SEQ = 4
N_TP = 2


def draw_projected(key, part):
    streams = jax.random.split(jax.random.fold_in(key, 11), 10)
    grid_shape = (2, TOKENS, H, HD)
    drawn = jnp.clip(jax.random.normal(streams[0], (3,) + grid_shape, jnp.float32), -4.5, 4.5)
    row_scale = jnp.exp(jax.random.uniform(streams[1], (2, TOKENS, H, 1), jnp.float32, math.log(0.3), math.log(3.0)))
    head_scale = jnp.exp(jax.random.uniform(streams[2], (2, 1, H, 1), jnp.float32, math.log(0.25), math.log(2.5)))
    jitter = jnp.exp(jax.random.uniform(streams[9], (2, TOKENS, H, 1), jnp.float32, math.log(0.9), math.log(1.1)))
    col_scale = head_scale * jitter
    queries = drawn[0] * row_scale
    key_rows = drawn[1] * col_scale
    values = drawn[2]
    stacked = jnp.stack([queries, key_rows, values], axis=2)
    return jnp.clip(stacked, -24.0, 24.0).reshape(2, TOKENS, 3, H * HD).astype(jnp.bfloat16)


def setup_inputs(seed: int = 0, part: int = 0) -> dict:
    arg_keys = jax.random.split(jax.random.key(seed), 5)
    part_keys = jax.random.split(jax.random.fold_in(arg_keys[4], part), 5)
    return {
        "projected": draw_projected(jax.random.fold_in(jax.random.fold_in(arg_keys[4], part), 71), part),
        "hint_gain": jnp.clip(jnp.exp(jax.random.uniform(arg_keys[1], (F,), jnp.float32, math.log(0.3), math.log(1.5))), 0.3, 1.5),
        "block_map": jax.random.permutation(arg_keys[2], N_SEQ).astype(jnp.int32),
        "token_perm": jax.vmap(lambda own: jax.random.permutation(own, TOK_DEV))(jax.random.split(arg_keys[3], (N_SEQ * N_TP))).reshape((N_SEQ * N_TP, TOK_DEV)).astype(jnp.int32),
    }


def reference(projected, hint_gain, block_map, token_perm):
    scaling = 1.0 / math.sqrt(HD)

    def single_head(position):
        branch = position // H
        head_index = position % H
        zero = jnp.zeros((), jnp.int32)
        sliced = lax.dynamic_slice(projected, (branch, zero, zero, head_index * HD), (1, TOKENS, 3, HD))[0]
        queries = sliced[:, 0].astype(jnp.float32)
        key_rows = sliced[:, 1].astype(jnp.float32)
        values = sliced[:, 2].astype(jnp.float32)
        scores = jnp.dot(queries, key_rows.T, precision=lax.Precision.HIGHEST, preferred_element_type=jnp.float32) * scaling
        highest = lax.optimization_barrier(jnp.max(scores, axis=1, keepdims=True))
        weights = jnp.exp(scores - highest)
        totals = lax.optimization_barrier(jnp.sum(weights, axis=1, keepdims=True))
        rounded = weights.astype(jnp.bfloat16).astype(jnp.float32)
        attended = jnp.dot(rounded, values, precision=lax.Precision.HIGHEST, preferred_element_type=jnp.float32) / totals
        return attended.astype(jnp.bfloat16)
    heads = lax.map(single_head, jnp.arange(2 * H, dtype=jnp.int32))
    attended = heads.reshape(2, H, TOKENS, HD).transpose(0, 2, 1, 3).reshape(2, TOKENS, H * HD)
    attended = lax.optimization_barrier(attended)
    positions = jnp.arange(TOKENS, dtype=jnp.int32)
    source = ROW * block_map[positions // ROW] + TOK_DEV * (positions % ROW // TOK_DEV) + token_perm[positions // TOK_DEV, positions % TOK_DEV]
    control = attended[1][source].astype(jnp.float32)
    base_out = (attended[0].astype(jnp.float32) + hint_gain * control).astype(jnp.bfloat16)
    return jnp.stack([base_out, attended[1]])
```

```python
import functools
import math

import jax
import jax.numpy as jnp
from jax import lax
from jax.experimental import pallas as pl
from jax.experimental.pallas import tpu as pltpu
from jax.sharding import PartitionSpec as P

HD = 128
GROUP = ("seq", "tp")
VMEM_LIMIT = 32 * 1024 * 1024

key_block = 512

SHARES = (1.0,)


def group_index():
    return lax.axis_index("seq") * lax.axis_size("tp") + lax.axis_index("tp")


def columns_of(group, step, width, start, size):
    first = lax.bitwise_xor(group, step) * width + start
    return pl.ds(pl.multiple_of(first, HD), size)


def split_kernel(chunks, count, width, rows_ref, *refs):
    outs, sems = refs[:-1], refs[-1]
    me = group_index()
    copies = []
    for c, (start, size) in enumerate(chunks):
        for step in range(count):
            n = c * count + step
            copies.append(
                pltpu.make_async_copy(
                    rows_ref.at[:, :, columns_of(me, step, width, start, size)],
                    outs[n],
                    sems.at[n],
                )
            )
    for copy in copies:
        copy.start()
    for copy in copies:
        copy.wait()


def attend_kernel(count, rows, size, *refs):
    pieces, out_ref = refs[:count], refs[count]
    scaling = 1.0 / math.sqrt(HD)
    for head in range(size // HD):
        at = slice(head * HD, (head + 1) * HD)
        queries, keys, values = (
            jnp.concatenate([piece[n, :, at] for piece in pieces], axis=0) for n in range(3)
        )
        scores = lax.dot_general(
            queries, keys, (((1,), (1,)), ((), ())), preferred_element_type=jnp.float32
        )
        highest = jnp.max(scores, axis=1, keepdims=True)
        weights = jnp.exp((scores - highest) * scaling)
        totals = jnp.sum(weights, axis=1, keepdims=True)
        summed = jnp.dot(
            weights.astype(jnp.bfloat16), values, preferred_element_type=jnp.float32
        )
        out_ref[:, :, at] = (summed / totals).astype(jnp.bfloat16).reshape(count, rows, HD)


def join_kernel(count, rows, width, start, size, map_ref, perm_ref, gain_ref, own_ref, hint_ref, *outs):
    me = group_index()
    tp_count = lax.axis_size("tp")
    gain = gain_ref[:, columns_of(me, 0, width, start, size)]
    gain = jnp.where(lax.axis_index("branch") == 0, gain, jnp.zeros_like(gain))
    source_row = lax.broadcasted_iota(jnp.int32, (rows, rows), 0)
    for step in range(count):
        block = lax.bitwise_xor(me, step)
        source = map_ref[block // tp_count] * tp_count + block % tp_count
        chosen = (source_row == perm_ref[pl.ds(block, 1), :]).astype(jnp.bfloat16)
        control = lax.dot_general(
            chosen,
            hint_ref[lax.bitwise_xor(source, me)],
            (((0,), (0,)), ((), ())),
            preferred_element_type=jnp.float32,
        )
        outs[step][...] = (own_ref[step].astype(jnp.float32) + gain * control).astype(jnp.bfloat16)


def merge_kernel(chunks, count, width, *refs):
    pieces, out_ref, sems = refs[:-2], refs[-2], refs[-1]
    me = group_index()
    copies = []
    for c, (start, size) in enumerate(chunks):
        for step in range(count):
            n = c * count + step
            copies.append(
                pltpu.make_async_copy(
                    pieces[n],
                    out_ref.at[:, columns_of(me, step, width, start, size)],
                    sems.at[n],
                )
            )
    for copy in copies:
        copy.start()
    for copy in copies:
        copy.wait()


def any_specs(number):
    return [pl.BlockSpec(memory_space=pl.ANY)] * number


def vmem_specs(number):
    return [pl.BlockSpec(memory_space=pltpu.VMEM)] * number


PARAMS = pltpu.CompilerParams(vmem_limit_bytes=VMEM_LIMIT)


def exchange(piece, step, count):
    if step == 0:
        return piece
    return lax.ppermute(piece, GROUP, [(i, i ^ step) for i in range(count)])


def by_heads(projected, hint_gain, block_map, token_perm):
    rows, features = projected.shape[1], projected.shape[3]
    count = lax.axis_size("seq") * lax.axis_size("tp")
    width = features // count
    heads = width // HD
    edges = [0]
    for share in SHARES:
        edges.append(min(heads, edges[-1] + max(1, round(share * heads))))
    edges[-1] = heads
    chunks = [(a * HD, (b - a) * HD) for a, b in zip(edges, edges[1:]) if b > a]
    stacked = jnp.transpose(projected[0], (1, 0, 2))
    sent = pl.pallas_call(
        functools.partial(split_kernel, chunks, count, width),
        out_shape=[
            jax.ShapeDtypeStruct((3, rows, size), projected.dtype)
            for start, size in chunks
            for step in range(count)
        ],
        in_specs=any_specs(1),
        out_specs=any_specs(len(chunks) * count),
        scratch_shapes=[pltpu.SemaphoreType.DMA((len(chunks) * count,))],
        compiler_params=PARAMS,
        name="split",
    )(stacked)
    gain = hint_gain[None, :]
    returned = []
    for c, (start, size) in enumerate(chunks):
        pieces = [exchange(sent[c * count + step], step, count) for step in range(count)]
        attended = pl.pallas_call(
            functools.partial(attend_kernel, count, rows, size),
            out_shape=jax.ShapeDtypeStruct((count, rows, size), projected.dtype),
            in_specs=vmem_specs(count),
            out_specs=vmem_specs(1)[0],
            compiler_params=PARAMS,
            name="attend",
        )(*pieces)
        hint = lax.ppermute(attended, "branch", [(1, 0)])
        joined = pl.pallas_call(
            functools.partial(join_kernel, count, rows, width, start, size),
            out_shape=[jax.ShapeDtypeStruct((rows, size), projected.dtype)] * count,
            in_specs=[pl.BlockSpec(memory_space=pltpu.SMEM)] + vmem_specs(4),
            out_specs=vmem_specs(count),
            compiler_params=PARAMS,
            name="join",
        )(block_map, token_perm, gain, attended, hint)
        returned += [exchange(joined[step], step, count) for step in range(count)]
    result = pl.pallas_call(
        functools.partial(merge_kernel, chunks, count, width),
        out_shape=jax.ShapeDtypeStruct((rows, features), projected.dtype),
        in_specs=any_specs(len(returned)),
        out_specs=any_specs(1)[0],
        scratch_shapes=[pltpu.SemaphoreType.DMA((len(returned),))],
        compiler_params=PARAMS,
        name="merge",
    )(*returned)
    return result[None]


def passed_along(x, axis, by):
    count = lax.axis_size(axis)
    pairs = [(i, i + by) for i in range(count) if 0 <= i + by < count]
    return lax.ppermute(x, axis, pairs)


def attend(queries, key_rows, value_rows):
    row_count, columns = queries.shape
    local_heads = columns // HD
    query_heads = queries.reshape(row_count, local_heads, HD)
    scaling = 1.0 / math.sqrt(HD)
    initial = (
        jnp.full((local_heads, row_count), -jnp.inf, jnp.float32),
        jnp.zeros((local_heads, row_count), jnp.float32),
        jnp.zeros((local_heads, row_count, HD), jnp.float32),
    )
    running = initial
    key_piece = lax.all_gather(key_rows, "tp", axis=0, tiled=True)
    value_piece = lax.all_gather(value_rows, "tp", axis=0, tiled=True)
    length = key_piece.shape[0]
    step_rows = key_block if length % key_block == 0 else length
    number = length // step_rows
    key_blocks = key_piece.reshape(number, step_rows, local_heads, HD)
    value_blocks = value_piece.reshape(number, step_rows, local_heads, HD)

    def update(carried, blocks_now):
        highest, totals, summed = carried
        key_now, value_now = blocks_now
        scores = (
            jnp.einsum("qhd,khd->hqk", query_heads, key_now, preferred_element_type=jnp.float32)
            * scaling
        )
        new_highest = jnp.maximum(highest, jnp.max(scores, axis=2))
        fading = jnp.exp(highest - new_highest)
        weights = jnp.exp(scores - new_highest[..., None])
        totals = totals * fading + jnp.sum(weights, axis=2)
        summed = summed * fading[..., None] + jnp.einsum(
            "hqk,khd->hqd",
            weights.astype(jnp.bfloat16),
            value_now,
            preferred_element_type=jnp.float32,
        )
        return ((new_highest, totals, summed), None)

    running, unused = lax.scan(update, running, (key_blocks, value_blocks))
    highest, totals, summed = running
    result = summed / totals[..., None]
    return jnp.transpose(result, (1, 0, 2)).reshape(row_count, columns).astype(jnp.bfloat16)


def by_heads_and_rows(projected, hint_gain, block_map, token_perm):
    block_rows = projected.shape[1]
    features = projected.shape[3]
    seq_count = lax.axis_size("seq")
    tp_count = lax.axis_size("tp")
    branch_index = lax.axis_index("branch")
    seq_index = lax.axis_index("seq")
    tp_index = lax.axis_index("tp")
    arrived = lax.all_to_all(projected[0], "seq", split_axis=2, concat_axis=0, tiled=True)
    columns = features // seq_count
    attended = attend(arrived[:, 0], arrived[:, 1], arrived[:, 2])
    attended = lax.optimization_barrier(attended)
    partner = passed_along(attended, "branch", -1)
    perm_table = token_perm.reshape(seq_count, tp_count, block_rows)
    column = lax.dynamic_index_in_dim(perm_table, tp_index, 1, keepdims=False)
    picked = (block_map[:, None] * block_rows + column).reshape(-1)
    control = jnp.take(partner, picked, axis=0).astype(jnp.float32)
    gain_slice = lax.dynamic_slice_in_dim(hint_gain, seq_index * columns, columns)
    summed = (attended.astype(jnp.float32) + gain_slice * control).astype(jnp.bfloat16)
    result = jnp.where(branch_index == 0, summed, attended)
    return lax.all_to_all(result, "seq", split_axis=0, concat_axis=1, tiled=True)[None]


def on_device(projected, hint_gain, block_map, token_perm):
    count = lax.axis_size("seq") * lax.axis_size("tp")
    rows, heads = projected.shape[1], projected.shape[3] // HD
    if heads % count == 0 and count & (count - 1) == 0 and rows % 16 == 0:
        return by_heads(projected, hint_gain, block_map, token_perm)
    return by_heads_and_rows(projected, hint_gain, block_map, token_perm)


def solution(mesh):
    return jax.shard_map(
        on_device,
        mesh=mesh,
        in_specs=(P("branch", ("req", "seq", "tp"), None, None), P(), P(), P()),
        out_specs=P("branch", ("req", "seq", "tp"), None),
        check_vma=False,
    )
```

```python
import functools
import math

import jax
import jax.numpy as jnp
from jax import lax
from jax.experimental import pallas as pl
from jax.experimental.pallas import tpu as pltpu
from jax.sharding import PartitionSpec as P

HD = 128
GROUP = ("seq", "tp")
VMEM_LIMIT = 32 * 1024 * 1024

key_block = 512

ORDER_IN = (4, 2, 6, 5, 3, 7, 1)
ORDER_BACK = (4, 6, 5, 7, 2, 3, 1)


def group_index():
    return lax.axis_index("seq") * lax.axis_size("tp") + lax.axis_index("tp")


def columns_of(group, step, width):
    return pl.ds(pl.multiple_of(lax.bitwise_xor(group, step) * width, HD), width)


def split_kernel(order, width, rows_ref, *refs):
    outs, sems = refs[:-1], refs[-1]
    me = group_index()
    copies = [
        pltpu.make_async_copy(
            rows_ref.at[:, :, columns_of(me, step, width)], outs[n], sems.at[n]
        )
        for n, step in enumerate(order)
    ]
    for copy in copies:
        copy.start()
    for copy in copies:
        copy.wait()


def attend_kernel(count, rows, width, *refs):
    pieces, out_ref = refs[:count], refs[count]
    scaling = 1.0 / math.sqrt(HD)
    for head in range(width // HD):
        at = slice(head * HD, (head + 1) * HD)
        queries, keys, values = (
            jnp.concatenate([piece[n, :, at] for piece in pieces], axis=0) for n in range(3)
        )
        scores = lax.dot_general(
            queries, keys, (((1,), (1,)), ((), ())), preferred_element_type=jnp.float32
        )
        highest = jnp.max(scores, axis=1, keepdims=True)
        weights = jnp.exp((scores - highest) * scaling)
        totals = jnp.sum(weights, axis=1, keepdims=True)
        summed = jnp.dot(
            weights.astype(jnp.bfloat16), values, preferred_element_type=jnp.float32
        )
        out_ref[:, :, at] = (summed / totals).astype(jnp.bfloat16).reshape(count, rows, HD)


def join_kernel(order_in, order, rows, width, map_ref, perm_ref, gain_ref, own_ref, hint_ref, *outs):
    me = group_index()
    tp_count = lax.axis_size("tp")
    gain = gain_ref[:, columns_of(me, 0, width)]
    gain = jnp.where(lax.axis_index("branch") == 0, gain, jnp.zeros_like(gain))
    source_row = lax.broadcasted_iota(jnp.int32, (rows, rows), 0)
    for n, step in enumerate(order):
        block = lax.bitwise_xor(me, step)
        source = map_ref[block // tp_count] * tp_count + block % tp_count
        distance = lax.bitwise_xor(source, me)
        place = sum(jnp.where(distance == far, at, 0) for at, far in enumerate(order_in))
        chosen = (source_row == perm_ref[pl.ds(block, 1), :]).astype(jnp.bfloat16)
        control = lax.dot_general(
            chosen, hint_ref[place], (((0,), (0,)), ((), ())), preferred_element_type=jnp.float32
        )
        own = own_ref[order_in.index(step)].astype(jnp.float32)
        outs[n][...] = (own + gain * control).astype(jnp.bfloat16)


def merge_kernel(order, width, *refs):
    pieces, out_ref, sems = refs[:-2], refs[-2], refs[-1]
    me = group_index()
    copies = [
        pltpu.make_async_copy(piece, out_ref.at[:, columns_of(me, step, width)], sems.at[n])
        for n, (step, piece) in enumerate(zip(order, pieces))
    ]
    for copy in copies:
        copy.start()
    for copy in copies:
        copy.wait()


def any_specs(number):
    return [pl.BlockSpec(memory_space=pl.ANY)] * number


def vmem_specs(number):
    return [pl.BlockSpec(memory_space=pltpu.VMEM)] * number


PARAMS = pltpu.CompilerParams(vmem_limit_bytes=VMEM_LIMIT)


def in_order(order, count):
    first = [step for step in order if step < count]
    return first + [step for step in range(1, count) if step not in first] + [0]


def exchange(pieces, order):
    pairs = lambda step: [(i, i ^ step) for i in range(len(order))]
    return [
        lax.ppermute(piece, GROUP, pairs(step)) if step else piece
        for step, piece in zip(order, pieces)
    ]


def by_heads(projected, hint_gain, block_map, token_perm):
    rows, features = projected.shape[1], projected.shape[3]
    count = lax.axis_size("seq") * lax.axis_size("tp")
    width = features // count
    order_in, order_back = in_order(ORDER_IN, count), in_order(ORDER_BACK, count)
    dtype = projected.dtype
    sent = pl.pallas_call(
        functools.partial(split_kernel, order_in, width),
        out_shape=[jax.ShapeDtypeStruct((3, rows, width), dtype)] * count,
        in_specs=any_specs(1),
        out_specs=any_specs(count),
        scratch_shapes=[pltpu.SemaphoreType.DMA((count,))],
        compiler_params=PARAMS,
        name="split",
    )(jnp.transpose(projected[0], (1, 0, 2)))
    attended = pl.pallas_call(
        functools.partial(attend_kernel, count, rows, width),
        out_shape=jax.ShapeDtypeStruct((count, rows, width), dtype),
        in_specs=vmem_specs(count),
        out_specs=vmem_specs(1)[0],
        compiler_params=PARAMS,
        name="attend",
    )(*exchange(sent, order_in))
    other = lax.ppermute(attended, "branch", [(0, 1), (1, 0)])
    joined = pl.pallas_call(
        functools.partial(join_kernel, order_in, order_back, rows, width),
        out_shape=[jax.ShapeDtypeStruct((rows, width), dtype)] * count,
        in_specs=[pl.BlockSpec(memory_space=pltpu.SMEM)] + vmem_specs(4),
        out_specs=vmem_specs(count),
        compiler_params=PARAMS,
        name="join",
    )(block_map, token_perm, hint_gain[None, :], attended, other)
    result = pl.pallas_call(
        functools.partial(merge_kernel, order_back, width),
        out_shape=jax.ShapeDtypeStruct((rows, features), dtype),
        in_specs=any_specs(count),
        out_specs=any_specs(1)[0],
        scratch_shapes=[pltpu.SemaphoreType.DMA((count,))],
        compiler_params=PARAMS,
        name="merge",
    )(*exchange(joined, order_back))
    return result[None]


def passed_along(x, axis, by):
    count = lax.axis_size(axis)
    pairs = [(i, i + by) for i in range(count) if 0 <= i + by < count]
    return lax.ppermute(x, axis, pairs)


def attend(queries, key_rows, value_rows):
    row_count, columns = queries.shape
    local_heads = columns // HD
    query_heads = queries.reshape(row_count, local_heads, HD)
    scaling = 1.0 / math.sqrt(HD)
    initial = (
        jnp.full((local_heads, row_count), -jnp.inf, jnp.float32),
        jnp.zeros((local_heads, row_count), jnp.float32),
        jnp.zeros((local_heads, row_count, HD), jnp.float32),
    )
    running = initial
    key_piece = lax.all_gather(key_rows, "tp", axis=0, tiled=True)
    value_piece = lax.all_gather(value_rows, "tp", axis=0, tiled=True)
    length = key_piece.shape[0]
    step_rows = key_block if length % key_block == 0 else length
    number = length // step_rows
    key_blocks = key_piece.reshape(number, step_rows, local_heads, HD)
    value_blocks = value_piece.reshape(number, step_rows, local_heads, HD)

    def update(carried, blocks_now):
        highest, totals, summed = carried
        key_now, value_now = blocks_now
        scores = (
            jnp.einsum("qhd,khd->hqk", query_heads, key_now, preferred_element_type=jnp.float32)
            * scaling
        )
        new_highest = jnp.maximum(highest, jnp.max(scores, axis=2))
        fading = jnp.exp(highest - new_highest)
        weights = jnp.exp(scores - new_highest[..., None])
        totals = totals * fading + jnp.sum(weights, axis=2)
        summed = summed * fading[..., None] + jnp.einsum(
            "hqk,khd->hqd",
            weights.astype(jnp.bfloat16),
            value_now,
            preferred_element_type=jnp.float32,
        )
        return ((new_highest, totals, summed), None)

    running, unused = lax.scan(update, running, (key_blocks, value_blocks))
    highest, totals, summed = running
    result = summed / totals[..., None]
    return jnp.transpose(result, (1, 0, 2)).reshape(row_count, columns).astype(jnp.bfloat16)


def by_heads_and_rows(projected, hint_gain, block_map, token_perm):
    block_rows = projected.shape[1]
    features = projected.shape[3]
    seq_count = lax.axis_size("seq")
    tp_count = lax.axis_size("tp")
    branch_index = lax.axis_index("branch")
    seq_index = lax.axis_index("seq")
    tp_index = lax.axis_index("tp")
    arrived = lax.all_to_all(projected[0], "seq", split_axis=2, concat_axis=0, tiled=True)
    columns = features // seq_count
    attended = attend(arrived[:, 0], arrived[:, 1], arrived[:, 2])
    attended = lax.optimization_barrier(attended)
    partner = passed_along(attended, "branch", -1)
    perm_table = token_perm.reshape(seq_count, tp_count, block_rows)
    column = lax.dynamic_index_in_dim(perm_table, tp_index, 1, keepdims=False)
    picked = (block_map[:, None] * block_rows + column).reshape(-1)
    control = jnp.take(partner, picked, axis=0).astype(jnp.float32)
    gain_slice = lax.dynamic_slice_in_dim(hint_gain, seq_index * columns, columns)
    summed = (attended.astype(jnp.float32) + gain_slice * control).astype(jnp.bfloat16)
    result = jnp.where(branch_index == 0, summed, attended)
    return lax.all_to_all(result, "seq", split_axis=0, concat_axis=1, tiled=True)[None]


def on_device(projected, hint_gain, block_map, token_perm):
    count = lax.axis_size("seq") * lax.axis_size("tp")
    rows, heads = projected.shape[1], projected.shape[3] // HD
    if heads % count == 0 and count & (count - 1) == 0 and rows % 16 == 0:
        return by_heads(projected, hint_gain, block_map, token_perm)
    return by_heads_and_rows(projected, hint_gain, block_map, token_perm)


def solution(mesh):
    return jax.shard_map(
        on_device,
        mesh=mesh,
        in_specs=(P("branch", ("req", "seq", "tp"), None, None), P(), P(), P()),
        out_specs=P("branch", ("req", "seq", "tp"), None),
        check_vma=False,
    )
```

```python
import functools
import math

import jax
import jax.numpy as jnp
from jax import lax
from jax.experimental import pallas as pl
from jax.experimental.pallas import tpu as pltpu
from jax.sharding import PartitionSpec as P

HD = 128
GROUP = ("seq", "tp")
VMEM_LIMIT = 32 * 1024 * 1024

key_block = 512

ORDER_IN = (6, 3, 2, 5, 4, 7, 1)
ORDER_BACK = (7, 6, 4, 5, 3, 2, 1)


def group_index():
    return lax.axis_index("seq") * lax.axis_size("tp") + lax.axis_index("tp")


def columns_of(group, step, width):
    return pl.ds(pl.multiple_of(lax.bitwise_xor(group, step) * width, HD), width)


def split_kernel(order, width, rows_ref, *refs):
    outs, sems = refs[:-1], refs[-1]
    me = group_index()
    copies = [
        pltpu.make_async_copy(
            rows_ref.at[:, :, columns_of(me, step, width)], outs[n], sems.at[n]
        )
        for n, step in enumerate(order)
    ]
    for copy in copies:
        copy.start()
    for copy in copies:
        copy.wait()


def attend_kernel(count, rows, width, *refs):
    pieces, out_ref = refs[:count], refs[count]
    scaling = 1.0 / math.sqrt(HD)
    heads = [slice(first, first + HD) for first in range(0, width, HD)]
    joined = lambda n, at: jnp.concatenate([piece[n, :, at] for piece in pieces], axis=0)
    scores = [
        lax.dot_general(
            joined(0, at),
            joined(1, at),
            (((1,), (1,)), ((), ())),
            preferred_element_type=jnp.float32,
        )
        for at in heads
    ]
    weighted = []
    for score in scores:
        highest = jnp.max(score, axis=1, keepdims=True)
        weights = jnp.exp((score - highest) * scaling)
        weighted.append((weights.astype(jnp.bfloat16), jnp.sum(weights, axis=1, keepdims=True)))
    for at, (probs, totals) in zip(heads, weighted):
        summed = jnp.dot(probs, joined(2, at), preferred_element_type=jnp.float32)
        out_ref[:, :, at] = (summed / totals).astype(jnp.bfloat16).reshape(count, rows, HD)


def choose_kernel(order_in, order, rows, map_ref, perm_ref, out_ref):
    me = group_index()
    tp_count = lax.axis_size("tp")
    tokens = len(order) * rows
    lane = lax.broadcasted_iota(jnp.int32, (1, tokens), 1)
    row_of = jnp.zeros((1, tokens), jnp.int32)
    first_of = jnp.zeros((1, tokens), jnp.int32)
    for n, step in enumerate(order):
        block = lax.bitwise_xor(me, step)
        source = map_ref[block // tp_count] * tp_count + block % tp_count
        distance = lax.bitwise_xor(source, me)
        place = sum(jnp.where(distance == far, at, 0) for at, far in enumerate(order_in))
        here = (lane >= n * rows) & (lane < (n + 1) * rows)
        row_of = jnp.where(here, block, row_of)
        first_of = jnp.where(here, place * rows, first_of)
    within = lax.broadcasted_iota(jnp.int32, (rows, tokens), 0)
    repeat = sum((within + n * rows == lane).astype(jnp.float32) for n in range(len(order)))
    perms = jnp.dot(
        perm_ref[...].astype(jnp.float32),
        repeat,
        precision=lax.Precision.HIGHEST,
        preferred_element_type=jnp.float32,
    )
    number = lax.broadcasted_iota(jnp.int32, perms.shape, 0)
    perm = jnp.sum(jnp.where(number == row_of, perms, 0.0), axis=0, keepdims=True)
    source_token = first_of.astype(jnp.float32) + perm
    column = lax.broadcasted_iota(jnp.int32, (tokens, tokens), 0).astype(jnp.float32)
    out_ref[...] = (column == source_token).astype(jnp.float32).T.astype(out_ref.dtype)


def join_kernel(order_in, order, rows, width, chosen_ref, gain_ref, own_ref, hint_ref, *outs):
    gain = gain_ref[:, columns_of(group_index(), 0, width)]
    gain = jnp.where(lax.axis_index("branch") == 0, gain, jnp.zeros_like(gain))
    control = jnp.dot(
        chosen_ref[...],
        hint_ref[...].reshape(len(order) * rows, width),
        preferred_element_type=jnp.float32,
    )
    for n, step in enumerate(order):
        own = own_ref[order_in.index(step)].astype(jnp.float32)
        added = gain * control[n * rows : (n + 1) * rows]
        outs[n][...] = (own + added).astype(jnp.bfloat16)


def merge_kernel(order, width, *refs):
    pieces, out_ref, sems = refs[:-2], refs[-2], refs[-1]
    me = group_index()
    copies = [
        pltpu.make_async_copy(piece, out_ref.at[:, columns_of(me, step, width)], sems.at[n])
        for n, (step, piece) in enumerate(zip(order, pieces))
    ]
    for copy in copies:
        copy.start()
    for copy in copies:
        copy.wait()


def any_specs(number):
    return [pl.BlockSpec(memory_space=pl.ANY)] * number


def vmem_specs(number):
    return [pl.BlockSpec(memory_space=pltpu.VMEM)] * number


PARAMS = pltpu.CompilerParams(vmem_limit_bytes=VMEM_LIMIT)


def in_order(order, count):
    first = [step for step in order if step < count]
    return first + [step for step in range(1, count) if step not in first] + [0]


def exchange(pieces, order):
    pairs = lambda step: [(i, i ^ step) for i in range(len(order))]
    return [
        lax.ppermute(piece, GROUP, pairs(step)) if step else piece
        for step, piece in zip(order, pieces)
    ]


def by_heads(projected, hint_gain, block_map, token_perm):
    rows, features = projected.shape[1], projected.shape[3]
    count = lax.axis_size("seq") * lax.axis_size("tp")
    width = features // count
    order_in, order_back = in_order(ORDER_IN, count), in_order(ORDER_BACK, count)
    dtype = projected.dtype
    sent = pl.pallas_call(
        functools.partial(split_kernel, order_in, width),
        out_shape=[jax.ShapeDtypeStruct((3, rows, width), dtype)] * count,
        in_specs=any_specs(1),
        out_specs=any_specs(count),
        scratch_shapes=[pltpu.SemaphoreType.DMA((count,))],
        compiler_params=PARAMS,
        name="split",
    )(jnp.transpose(projected[0], (1, 0, 2)))
    arrived = exchange(sent, order_in)
    attended = pl.pallas_call(
        functools.partial(attend_kernel, count, rows, width),
        out_shape=jax.ShapeDtypeStruct((count, rows, width), dtype),
        in_specs=vmem_specs(count),
        out_specs=vmem_specs(1)[0],
        compiler_params=PARAMS,
        name="attend",
    )(*arrived)
    other = lax.ppermute(attended, "branch", [(0, 1), (1, 0)])
    block_map, attended = lax.optimization_barrier((block_map, attended))
    tokens = count * rows
    chosen = pl.pallas_call(
        functools.partial(choose_kernel, order_in, order_back, rows),
        out_shape=jax.ShapeDtypeStruct((tokens, tokens), dtype),
        in_specs=[pl.BlockSpec(memory_space=pltpu.SMEM)] + vmem_specs(1),
        out_specs=vmem_specs(1)[0],
        compiler_params=PARAMS,
        name="choose",
    )(block_map, token_perm)
    joined = pl.pallas_call(
        functools.partial(join_kernel, order_in, order_back, rows, width),
        out_shape=[jax.ShapeDtypeStruct((rows, width), dtype)] * count,
        in_specs=vmem_specs(4),
        out_specs=vmem_specs(count),
        compiler_params=PARAMS,
        name="join",
    )(chosen, hint_gain[None, :], attended, other)
    result = pl.pallas_call(
        functools.partial(merge_kernel, order_back, width),
        out_shape=jax.ShapeDtypeStruct((rows, features), dtype),
        in_specs=any_specs(count),
        out_specs=any_specs(1)[0],
        scratch_shapes=[pltpu.SemaphoreType.DMA((count,))],
        compiler_params=PARAMS,
        name="merge",
    )(*exchange(joined, order_back))
    return result[None]


def passed_along(x, axis, by):
    count = lax.axis_size(axis)
    pairs = [(i, i + by) for i in range(count) if 0 <= i + by < count]
    return lax.ppermute(x, axis, pairs)


def attend(queries, key_rows, value_rows):
    row_count, columns = queries.shape
    local_heads = columns // HD
    query_heads = queries.reshape(row_count, local_heads, HD)
    scaling = 1.0 / math.sqrt(HD)
    initial = (
        jnp.full((local_heads, row_count), -jnp.inf, jnp.float32),
        jnp.zeros((local_heads, row_count), jnp.float32),
        jnp.zeros((local_heads, row_count, HD), jnp.float32),
    )
    running = initial
    key_piece = lax.all_gather(key_rows, "tp", axis=0, tiled=True)
    value_piece = lax.all_gather(value_rows, "tp", axis=0, tiled=True)
    length = key_piece.shape[0]
    step_rows = key_block if length % key_block == 0 else length
    number = length // step_rows
    key_blocks = key_piece.reshape(number, step_rows, local_heads, HD)
    value_blocks = value_piece.reshape(number, step_rows, local_heads, HD)

    def update(carried, blocks_now):
        highest, totals, summed = carried
        key_now, value_now = blocks_now
        scores = (
            jnp.einsum("qhd,khd->hqk", query_heads, key_now, preferred_element_type=jnp.float32)
            * scaling
        )
        new_highest = jnp.maximum(highest, jnp.max(scores, axis=2))
        fading = jnp.exp(highest - new_highest)
        weights = jnp.exp(scores - new_highest[..., None])
        totals = totals * fading + jnp.sum(weights, axis=2)
        summed = summed * fading[..., None] + jnp.einsum(
            "hqk,khd->hqd",
            weights.astype(jnp.bfloat16),
            value_now,
            preferred_element_type=jnp.float32,
        )
        return ((new_highest, totals, summed), None)

    running, unused = lax.scan(update, running, (key_blocks, value_blocks))
    highest, totals, summed = running
    result = summed / totals[..., None]
    return jnp.transpose(result, (1, 0, 2)).reshape(row_count, columns).astype(jnp.bfloat16)


def by_heads_and_rows(projected, hint_gain, block_map, token_perm):
    block_rows = projected.shape[1]
    features = projected.shape[3]
    seq_count = lax.axis_size("seq")
    tp_count = lax.axis_size("tp")
    branch_index = lax.axis_index("branch")
    seq_index = lax.axis_index("seq")
    tp_index = lax.axis_index("tp")
    arrived = lax.all_to_all(projected[0], "seq", split_axis=2, concat_axis=0, tiled=True)
    columns = features // seq_count
    attended = attend(arrived[:, 0], arrived[:, 1], arrived[:, 2])
    attended = lax.optimization_barrier(attended)
    partner = passed_along(attended, "branch", -1)
    perm_table = token_perm.reshape(seq_count, tp_count, block_rows)
    column = lax.dynamic_index_in_dim(perm_table, tp_index, 1, keepdims=False)
    picked = (block_map[:, None] * block_rows + column).reshape(-1)
    control = jnp.take(partner, picked, axis=0).astype(jnp.float32)
    gain_slice = lax.dynamic_slice_in_dim(hint_gain, seq_index * columns, columns)
    summed = (attended.astype(jnp.float32) + gain_slice * control).astype(jnp.bfloat16)
    result = jnp.where(branch_index == 0, summed, attended)
    return lax.all_to_all(result, "seq", split_axis=0, concat_axis=1, tiled=True)[None]


def on_device(projected, hint_gain, block_map, token_perm):
    count = lax.axis_size("seq") * lax.axis_size("tp")
    rows, heads = projected.shape[1], projected.shape[3] // HD
    if heads % count == 0 and count & (count - 1) == 0 and rows % 16 == 0:
        return by_heads(projected, hint_gain, block_map, token_perm)
    return by_heads_and_rows(projected, hint_gain, block_map, token_perm)


def solution(mesh):
    return jax.shard_map(
        on_device,
        mesh=mesh,
        in_specs=(P("branch", ("req", "seq", "tp"), None, None), P(), P(), P()),
        out_specs=P("branch", ("req", "seq", "tp"), None),
        check_vma=False,
    )
```

```python
import functools
import math

import jax
import jax.numpy as jnp
from jax import lax
from jax.experimental import pallas as pl
from jax.experimental.pallas import tpu as pltpu
from jax.sharding import PartitionSpec as P

HD = 128
VMEM_LIMIT = 32 * 1024 * 1024

key_block = 512

ORDER_IN = ((6, 3, 2, 5, 4, 7, 1), (6, 3, 2, 5, 4, 7, 1))
ORDER_BACK = ((7, 3, 1, 0), (4, 6, 2, 5))


def group_index():
    return lax.axis_index("seq") * lax.axis_size("tp") + lax.axis_index("tp")


def columns_of(group, step, width):
    return pl.ds(pl.multiple_of(lax.bitwise_xor(group, step) * width, HD), width)


def split_kernel(orders, width, rows_ref, *refs):
    outs, sems = refs[:-1], refs[-1]
    me = group_index()
    copies = []
    for n, steps in enumerate(zip(*orders)):
        step = jnp.where(lax.axis_index("branch") == 0, *steps)
        piece = rows_ref.at[:, :, columns_of(me, step, width)]
        copies.append(pltpu.make_async_copy(piece, outs[n], sems.at[n]))
    for copy in copies:
        copy.start()
    for copy in copies:
        copy.wait()


def attend_kernel(count, rows, width, *refs):
    pieces, out_ref = refs[:count], refs[count]
    scaling = math.log2(math.e) / math.sqrt(HD)
    heads = [slice(first, first + HD) for first in range(0, width, HD)]
    joined = lambda n, at: jnp.concatenate([piece[n, :, at] for piece in pieces], axis=0)
    scores = [
        lax.dot_general(
            joined(0, at),
            joined(1, at),
            (((1,), (1,)), ((), ())),
            preferred_element_type=jnp.float32,
        )
        for at in heads
    ]
    weighted = []
    for score in scores:
        highest = jnp.max(score, axis=1, keepdims=True)
        weights = jnp.exp2((score - highest) * scaling)
        weighted.append((weights.astype(jnp.bfloat16), jnp.sum(weights, axis=1, keepdims=True)))
    for at, (probs, totals) in zip(heads, weighted):
        summed = jnp.dot(probs, joined(2, at), preferred_element_type=jnp.float32)
        out_ref[:, :, at] = (summed / totals).astype(jnp.bfloat16).reshape(count, rows, HD)


def on_branch(work):
    for branch in range(2):
        pl.when(lax.axis_index("branch") == branch)(functools.partial(work, branch))


def choose_kernel(orders_in, orders, rows, map_ref, perm_ref, out_ref):
    on_branch(lambda branch: choose(orders_in[1], orders[branch], rows, map_ref, perm_ref, out_ref))


def choose(order_in, order, rows, map_ref, perm_ref, out_ref):
    me = group_index()
    tp_count = lax.axis_size("tp")
    tokens = len(order) * rows
    lane = lax.broadcasted_iota(jnp.int32, (1, tokens), 1)
    row_of = jnp.zeros((1, tokens), jnp.int32)
    first_of = jnp.zeros((1, tokens), jnp.int32)
    for n, step in enumerate(order):
        block = lax.bitwise_xor(me, step)
        source = map_ref[block // tp_count] * tp_count + block % tp_count
        distance = lax.bitwise_xor(source, me)
        place = sum(jnp.where(distance == far, at, 0) for at, far in enumerate(order_in))
        here = (lane >= n * rows) & (lane < (n + 1) * rows)
        row_of = jnp.where(here, block, row_of)
        first_of = jnp.where(here, place * rows, first_of)
    within = lax.broadcasted_iota(jnp.int32, (rows, tokens), 0)
    repeat = sum((within + n * rows == lane).astype(jnp.float32) for n in range(len(order)))
    perms = jnp.dot(
        perm_ref[...].astype(jnp.float32),
        repeat,
        precision=lax.Precision.HIGHEST,
        preferred_element_type=jnp.float32,
    )
    number = lax.broadcasted_iota(jnp.int32, perms.shape, 0)
    perm = jnp.sum(jnp.where(number == row_of, perms, 0.0), axis=0, keepdims=True)
    source_token = first_of.astype(jnp.float32) + perm
    shape = (len(order_in) * rows, tokens)
    column = lax.broadcasted_iota(jnp.int32, shape, 0).astype(jnp.float32)
    out_ref[...] = (column == source_token).astype(jnp.float32).T.astype(out_ref.dtype)


def join_kernel(orders_in, orders, rows, width, chosen_ref, gain_ref, own_ref, other_ref, *outs):
    def work(branch):
        base_ref, control_ref = (own_ref, other_ref) if branch == 0 else (other_ref, own_ref)
        gain = gain_ref[:, columns_of(group_index(), 0, width)]
        hint = jnp.dot(
            chosen_ref[...],
            control_ref[...].reshape(len(orders_in[1]) * rows, width),
            preferred_element_type=jnp.float32,
        )
        for n, step in enumerate(orders[branch]):
            base = base_ref[orders_in[0].index(step)].astype(jnp.float32)
            added = gain * hint[n * rows : (n + 1) * rows]
            outs[n][branch] = (base + added).astype(jnp.bfloat16)
            outs[n][1 - branch] = control_ref[orders_in[1].index(step)]

    on_branch(work)


def take_kernel(in_ref, out_ref):
    out_ref[...] = in_ref[1]


def merge_kernel(orders, width, *refs):
    out_ref, sems = refs[-2:]
    count = len(orders[0])

    def work(branch):
        me = group_index()
        copies = []
        for n in range(count):
            for piece, step in (
                (refs[n].at[0], orders[branch][n]),
                (refs[count + n], orders[1 - branch][n]),
            ):
                place = out_ref.at[:, columns_of(me, step, width)]
                copies.append(pltpu.make_async_copy(piece, place, sems.at[len(copies)]))
        for copy in copies:
            copy.start()
        for copy in copies:
            copy.wait()

    on_branch(work)


def any_specs(number):
    return [pl.BlockSpec(memory_space=pl.ANY)] * number


def vmem_specs(number):
    return [pl.BlockSpec(memory_space=pltpu.VMEM)] * number


PARAMS = pltpu.CompilerParams(vmem_limit_bytes=VMEM_LIMIT)


def in_order(order, count):
    first = [step for step in order if step < count]
    return first + [step for step in range(1, count) if step not in first] + [0]


def halves(orders, count):
    known = [[step for step in order if step < count] for order in orders]
    for step in range(count):
        if step not in known[0] + known[1]:
            min(known, key=len).append(step)
    return known


def exchange_by_core(pieces, orders):
    tp_count = lax.axis_size("tp")
    groups = range(lax.axis_size("seq") * tp_count)
    device = lambda group, core: (group // tp_count * 2 + core) * tp_count + group % tp_count
    arrived = []
    for piece, steps in zip(pieces, zip(*orders)):
        pairs = [(device(g, core), device(g ^ steps[core], core)) for g in groups for core in (0, 1)]
        moved = any(steps)
        arrived.append(lax.ppermute(piece, ("seq", "branch", "tp"), pairs) if moved else piece)
    return arrived


def by_heads(projected, hint_gain, block_map, token_perm):
    rows, features = projected.shape[1], projected.shape[3]
    count = lax.axis_size("seq") * lax.axis_size("tp")
    width = features // count
    orders_in = [in_order(order, count) for order in ORDER_IN]
    orders_back = halves(ORDER_BACK, count)
    half = count // 2
    tokens = count * rows
    dtype = projected.dtype
    both = [(0, 1), (1, 0)]
    sent = pl.pallas_call(
        functools.partial(split_kernel, orders_in, width),
        out_shape=[jax.ShapeDtypeStruct((3, rows, width), dtype)] * count,
        in_specs=any_specs(1),
        out_specs=any_specs(count),
        scratch_shapes=[pltpu.SemaphoreType.DMA((count,))],
        compiler_params=PARAMS,
        name="split",
    )(jnp.transpose(projected[0], (1, 0, 2)))
    attended = pl.pallas_call(
        functools.partial(attend_kernel, count, rows, width),
        out_shape=jax.ShapeDtypeStruct((count, rows, width), dtype),
        in_specs=vmem_specs(count),
        out_specs=vmem_specs(1)[0],
        compiler_params=PARAMS,
        name="attend",
    )(*exchange_by_core(sent, orders_in))
    other = lax.ppermute(attended, "branch", both)
    block_map, attended = lax.optimization_barrier((block_map, attended))
    chosen = pl.pallas_call(
        functools.partial(choose_kernel, orders_in, orders_back, rows),
        out_shape=jax.ShapeDtypeStruct((half * rows, tokens), dtype),
        in_specs=[pl.BlockSpec(memory_space=pltpu.SMEM)] + vmem_specs(1),
        out_specs=vmem_specs(1)[0],
        compiler_params=PARAMS,
        name="choose",
    )(block_map, token_perm)
    joined = pl.pallas_call(
        functools.partial(join_kernel, orders_in, orders_back, rows, width),
        out_shape=[jax.ShapeDtypeStruct((2, rows, width), dtype)] * half,
        in_specs=vmem_specs(4),
        out_specs=vmem_specs(half),
        compiler_params=PARAMS,
        name="join",
    )(chosen, hint_gain[None, :], attended, other)
    returned = exchange_by_core(joined, orders_back)
    passed = []
    for piece in returned:
        taken = pl.pallas_call(
            take_kernel,
            out_shape=jax.ShapeDtypeStruct((rows, width), dtype),
            in_specs=vmem_specs(1),
            out_specs=vmem_specs(1)[0],
            compiler_params=PARAMS,
            name="take",
        )(piece)
        passed.append(lax.ppermute(taken, "branch", both))
    result = pl.pallas_call(
        functools.partial(merge_kernel, orders_back, width),
        out_shape=jax.ShapeDtypeStruct((rows, features), dtype),
        in_specs=any_specs(count),
        out_specs=any_specs(1)[0],
        scratch_shapes=[pltpu.SemaphoreType.DMA((count,))],
        compiler_params=PARAMS,
        name="merge",
    )(*returned, *passed)
    return result[None]


def passed_along(x, axis, by):
    count = lax.axis_size(axis)
    pairs = [(i, i + by) for i in range(count) if 0 <= i + by < count]
    return lax.ppermute(x, axis, pairs)


def attend(queries, key_rows, value_rows):
    row_count, columns = queries.shape
    local_heads = columns // HD
    query_heads = queries.reshape(row_count, local_heads, HD)
    scaling = 1.0 / math.sqrt(HD)
    initial = (
        jnp.full((local_heads, row_count), -jnp.inf, jnp.float32),
        jnp.zeros((local_heads, row_count), jnp.float32),
        jnp.zeros((local_heads, row_count, HD), jnp.float32),
    )
    running = initial
    key_piece = lax.all_gather(key_rows, "tp", axis=0, tiled=True)
    value_piece = lax.all_gather(value_rows, "tp", axis=0, tiled=True)
    length = key_piece.shape[0]
    step_rows = key_block if length % key_block == 0 else length
    number = length // step_rows
    key_blocks = key_piece.reshape(number, step_rows, local_heads, HD)
    value_blocks = value_piece.reshape(number, step_rows, local_heads, HD)

    def update(carried, blocks_now):
        highest, totals, summed = carried
        key_now, value_now = blocks_now
        scores = (
            jnp.einsum("qhd,khd->hqk", query_heads, key_now, preferred_element_type=jnp.float32)
            * scaling
        )
        new_highest = jnp.maximum(highest, jnp.max(scores, axis=2))
        fading = jnp.exp(highest - new_highest)
        weights = jnp.exp(scores - new_highest[..., None])
        totals = totals * fading + jnp.sum(weights, axis=2)
        summed = summed * fading[..., None] + jnp.einsum(
            "hqk,khd->hqd",
            weights.astype(jnp.bfloat16),
            value_now,
            preferred_element_type=jnp.float32,
        )
        return ((new_highest, totals, summed), None)

    running, unused = lax.scan(update, running, (key_blocks, value_blocks))
    highest, totals, summed = running
    result = summed / totals[..., None]
    return jnp.transpose(result, (1, 0, 2)).reshape(row_count, columns).astype(jnp.bfloat16)


def by_heads_and_rows(projected, hint_gain, block_map, token_perm):
    block_rows = projected.shape[1]
    features = projected.shape[3]
    seq_count = lax.axis_size("seq")
    tp_count = lax.axis_size("tp")
    branch_index = lax.axis_index("branch")
    seq_index = lax.axis_index("seq")
    tp_index = lax.axis_index("tp")
    arrived = lax.all_to_all(projected[0], "seq", split_axis=2, concat_axis=0, tiled=True)
    columns = features // seq_count
    attended = attend(arrived[:, 0], arrived[:, 1], arrived[:, 2])
    attended = lax.optimization_barrier(attended)
    partner = passed_along(attended, "branch", -1)
    perm_table = token_perm.reshape(seq_count, tp_count, block_rows)
    column = lax.dynamic_index_in_dim(perm_table, tp_index, 1, keepdims=False)
    picked = (block_map[:, None] * block_rows + column).reshape(-1)
    control = jnp.take(partner, picked, axis=0).astype(jnp.float32)
    gain_slice = lax.dynamic_slice_in_dim(hint_gain, seq_index * columns, columns)
    summed = (attended.astype(jnp.float32) + gain_slice * control).astype(jnp.bfloat16)
    result = jnp.where(branch_index == 0, summed, attended)
    return lax.all_to_all(result, "seq", split_axis=0, concat_axis=1, tiled=True)[None]


def on_device(projected, hint_gain, block_map, token_perm):
    count = lax.axis_size("seq") * lax.axis_size("tp")
    rows, heads = projected.shape[1], projected.shape[3] // HD
    if heads % count == 0 and count & (count - 1) == 0 and rows % 16 == 0:
        return by_heads(projected, hint_gain, block_map, token_perm)
    return by_heads_and_rows(projected, hint_gain, block_map, token_perm)


def solution(mesh):
    return jax.shard_map(
        on_device,
        mesh=mesh,
        in_specs=(P("branch", ("req", "seq", "tp"), None, None), P(), P(), P()),
        out_specs=P("branch", ("req", "seq", "tp"), None),
        check_vma=False,
    )
```

```python
import functools
import math

import jax
import jax.numpy as jnp
from jax import lax
from jax.experimental import pallas as pl
from jax.experimental.pallas import tpu as pltpu
from jax.sharding import PartitionSpec as P

HD = 128
VMEM_LIMIT = 32 * 1024 * 1024

key_block = 512

ORDER_IN = ((4, 3, 2, 5, 6, 7, 1), (6, 1, 2, 4, 5, 7, 3))
ORDER_BACK = ((6, 3, 1), (7, 5, 2))
STRAIGHT = (4,)
STRAIGHT_FIRST = False


def group_index():
    return lax.axis_index("seq") * lax.axis_size("tp") + lax.axis_index("tp")


def columns_of(group, step, width):
    return pl.ds(pl.multiple_of(lax.bitwise_xor(group, step) * width, HD), width)


def split_kernel(orders, width, rows_ref, *refs):
    outs, sems = refs[:-1], refs[-1]
    me = group_index()
    copies = []
    for n, steps in enumerate(zip(*orders)):
        step = jnp.where(lax.axis_index("branch") == 0, *steps)
        piece = rows_ref.at[:, :, columns_of(me, step, width)]
        copies.append(pltpu.make_async_copy(piece, outs[n], sems.at[n]))
    for copy in copies:
        copy.start()
    for copy in copies:
        copy.wait()


def attend_kernel(count, rows, start, stop, *refs):
    pieces, out_ref = refs[:count], refs[count]
    scaling = math.log2(math.e) / math.sqrt(HD)
    heads = [slice(first, first + HD) for first in range(start, stop, HD)]
    joined = lambda n, at: jnp.concatenate([piece[n, :, at] for piece in pieces], axis=0)
    scores = [
        lax.dot_general(
            joined(0, at),
            joined(1, at),
            (((1,), (1,)), ((), ())),
            preferred_element_type=jnp.float32,
        )
        for at in heads
    ]
    weighted = []
    for score in scores:
        highest = jnp.max(score, axis=1, keepdims=True)
        weights = jnp.exp2((score - highest) * scaling)
        weighted.append((weights.astype(jnp.bfloat16), jnp.sum(weights, axis=1, keepdims=True)))
    for at, (probs, totals) in zip(heads, weighted):
        summed = jnp.dot(probs, joined(2, at), preferred_element_type=jnp.float32)
        place = slice(at.start - start, at.stop - start)
        out_ref[:, :, place] = (summed / totals).astype(jnp.bfloat16).reshape(count, rows, HD)


def on_branch(work):
    for branch in range(2):
        pl.when(lax.axis_index("branch") == branch)(functools.partial(work, branch))


def choose_kernel(orders_in, orders, rows, map_ref, perm_ref, out_ref):
    on_branch(lambda branch: choose(orders_in[1], orders[branch], rows, map_ref, perm_ref, out_ref))


def choose(order_in, order, rows, map_ref, perm_ref, out_ref):
    me = group_index()
    tp_count = lax.axis_size("tp")
    tokens = len(order) * rows
    lane = lax.broadcasted_iota(jnp.int32, (1, tokens), 1)
    row_of = jnp.zeros((1, tokens), jnp.int32)
    first_of = jnp.zeros((1, tokens), jnp.int32)
    for n, step in enumerate(order):
        block = lax.bitwise_xor(me, step)
        source = map_ref[block // tp_count] * tp_count + block % tp_count
        distance = lax.bitwise_xor(source, me)
        place = sum(jnp.where(distance == far, at, 0) for at, far in enumerate(order_in))
        here = (lane >= n * rows) & (lane < (n + 1) * rows)
        row_of = jnp.where(here, block, row_of)
        first_of = jnp.where(here, place * rows, first_of)
    within = lax.broadcasted_iota(jnp.int32, (rows, tokens), 0)
    repeat = sum((within + n * rows == lane).astype(jnp.float32) for n in range(len(order)))
    perms = jnp.dot(
        perm_ref[...].astype(jnp.float32),
        repeat,
        precision=lax.Precision.HIGHEST,
        preferred_element_type=jnp.float32,
    )
    number = lax.broadcasted_iota(jnp.int32, perms.shape, 0)
    perm = jnp.sum(jnp.where(number == row_of, perms, 0.0), axis=0, keepdims=True)
    source_token = first_of.astype(jnp.float32) + perm
    shape = (len(order_in) * rows, tokens)
    column = lax.broadcasted_iota(jnp.int32, shape, 0).astype(jnp.float32)
    out_ref[...] = (column == source_token).astype(jnp.float32).T.astype(out_ref.dtype)


def join_kernel(orders_in, orders, straight, rows, width, chosen_ref, gain_ref, own_refs, other_refs, *outs):
    def work(branch):
        base_refs, control_refs = (own_refs, other_refs) if branch == 0 else (other_refs, own_refs)
        start = 0
        for base_ref, control_ref in zip(base_refs, control_refs):
            stop = start + base_ref.shape[2]
            at = slice(start, stop)
            gain = gain_ref[:, at]
            hint = jnp.dot(
                chosen_ref[...],
                control_ref[...].reshape(len(orders_in[1]) * rows, stop - start),
                preferred_element_type=jnp.float32,
            )
            for n, step in enumerate(orders[branch] + straight + [0]):
                control = control_ref[orders_in[1].index(step)]
                base = base_ref[orders_in[0].index(step)].astype(jnp.float32)
                added = gain * hint[n * rows : (n + 1) * rows]
                joined = (base + added).astype(jnp.bfloat16)
                if n < len(orders[branch]):
                    outs[n][branch, :, at] = joined
                    outs[n][1 - branch, :, at] = control
                else:
                    outs[n][:, at] = joined if branch == 0 else control
            start = stop

    on_branch(work)


def take_kernel(in_ref, out_ref):
    out_ref[...] = in_ref[1]


def merge_kernel(orders, straight, width, *refs):
    out_ref, sems = refs[-2:]
    if STRAIGHT_FIRST:
        own_refs, pair_refs, passed_refs = refs[:-2]
    else:
        pair_refs, passed_refs, own_refs = refs[:-2]

    def work(branch):
        me = group_index()
        pieces = [(ref.at[0], step) for ref, step in zip(pair_refs, orders[branch])]
        pieces += zip(passed_refs, orders[1 - branch])
        pieces += zip(own_refs, straight + [0])
        copies = []
        for n, (piece, step) in enumerate(pieces):
            place = out_ref.at[:, columns_of(me, step, width)]
            copies.append(pltpu.make_async_copy(piece, place, sems.at[n]))
        for copy in copies:
            copy.start()
        for copy in copies:
            copy.wait()

    on_branch(work)


def any_specs(number):
    return [pl.BlockSpec(memory_space=pl.ANY)] * number


def vmem_specs(number):
    return [pl.BlockSpec(memory_space=pltpu.VMEM)] * number


PARAMS = pltpu.CompilerParams(vmem_limit_bytes=VMEM_LIMIT)


def in_order(order, count):
    first = [step for step in order if step < count]
    return first + [step for step in range(1, count) if step not in first] + [0]


def back_plan(count):
    orders, straight = [list(order) for order in ORDER_BACK], list(STRAIGHT)
    steps = list(range(1, count))
    if sorted(orders[0] + orders[1] + straight) != steps:
        half = len(steps) // 2
        orders, straight = [steps[:half], steps[half : 2 * half]], steps[2 * half :]
    return orders, straight


def exchange_by_core(pieces, orders):
    tp_count = lax.axis_size("tp")
    groups = range(lax.axis_size("seq") * tp_count)
    device = lambda group, core: (group // tp_count * 2 + core) * tp_count + group % tp_count
    arrived = []
    for piece, steps in zip(pieces, zip(*orders)):
        pairs = [(device(g, core), device(g ^ steps[core], core)) for g in groups for core in (0, 1)]
        moved = any(steps)
        arrived.append(lax.ppermute(piece, ("seq", "branch", "tp"), pairs) if moved else piece)
    return arrived


def by_heads(projected, hint_gain, block_map, token_perm):
    rows, features = projected.shape[1], projected.shape[3]
    count = lax.axis_size("seq") * lax.axis_size("tp")
    width = features // count
    orders_in = [in_order(order, count) for order in ORDER_IN]
    orders_back, straight = back_plan(count)
    pairs = len(orders_back[0])
    stays = len(straight) + 1
    middle = width // HD // 2 * HD
    parts = [(0, width)]
    dtype = projected.dtype
    both = [(0, 1), (1, 0)]
    sent = pl.pallas_call(
        functools.partial(split_kernel, orders_in, width),
        out_shape=[jax.ShapeDtypeStruct((3, rows, width), dtype)] * count,
        in_specs=any_specs(1),
        out_specs=any_specs(count),
        scratch_shapes=[pltpu.SemaphoreType.DMA((count,))],
        compiler_params=PARAMS,
        name="split",
    )(jnp.transpose(projected[0], (1, 0, 2)))
    arrived = exchange_by_core(sent, orders_in)
    attended = [
        pl.pallas_call(
            functools.partial(attend_kernel, count, rows, start, stop),
            out_shape=jax.ShapeDtypeStruct((count, rows, stop - start), dtype),
            in_specs=vmem_specs(count),
            out_specs=vmem_specs(1)[0],
            compiler_params=PARAMS,
            name="attend",
        )(*arrived)
        for start, stop in parts
    ]
    other = [lax.ppermute(part, "branch", both) for part in attended]
    block_map, attended[-1] = lax.optimization_barrier((block_map, attended[-1]))
    chosen = pl.pallas_call(
        functools.partial(choose_kernel, orders_in, [order + straight + [0] for order in orders_back], rows),
        out_shape=jax.ShapeDtypeStruct(((pairs + stays) * rows, count * rows), dtype),
        in_specs=[pl.BlockSpec(memory_space=pltpu.SMEM)] + vmem_specs(1),
        out_specs=vmem_specs(1)[0],
        compiler_params=PARAMS,
        name="choose",
    )(block_map, token_perm)
    gain = lax.dynamic_slice_in_dim(hint_gain, group_index() * width, width)[None, :]
    joined = pl.pallas_call(
        functools.partial(join_kernel, orders_in, orders_back, straight, rows, width),
        out_shape=[jax.ShapeDtypeStruct((2, rows, width), dtype)] * pairs
        + [jax.ShapeDtypeStruct((rows, width), dtype)] * stays,
        in_specs=vmem_specs(2) + [vmem_specs(len(parts))] * 2,
        out_specs=vmem_specs(pairs + stays),
        compiler_params=PARAMS,
        name="join",
    )(chosen, gain, attended, other)
    returned = exchange_by_core(joined, [order + straight + [0] for order in orders_back])
    passed = []
    for piece in returned[:pairs]:
        taken = pl.pallas_call(
            take_kernel,
            out_shape=jax.ShapeDtypeStruct((rows, width), dtype),
            in_specs=vmem_specs(1),
            out_specs=vmem_specs(1)[0],
            compiler_params=PARAMS,
            name="take",
        )(piece)
        passed.append(lax.ppermute(taken, "branch", both))
    groups = [returned[:pairs], passed]
    groups.insert(0 if STRAIGHT_FIRST else 2, returned[pairs:])
    result = pl.pallas_call(
        functools.partial(merge_kernel, orders_back, straight, width),
        out_shape=jax.ShapeDtypeStruct((rows, features), dtype),
        in_specs=[any_specs(len(group)) for group in groups],
        out_specs=any_specs(1)[0],
        scratch_shapes=[pltpu.SemaphoreType.DMA((count,))],
        compiler_params=PARAMS,
        name="merge",
    )(*groups)
    return result[None]


def passed_along(x, axis, by):
    count = lax.axis_size(axis)
    pairs = [(i, i + by) for i in range(count) if 0 <= i + by < count]
    return lax.ppermute(x, axis, pairs)


def attend(queries, key_rows, value_rows):
    row_count, columns = queries.shape
    local_heads = columns // HD
    query_heads = queries.reshape(row_count, local_heads, HD)
    scaling = 1.0 / math.sqrt(HD)
    initial = (
        jnp.full((local_heads, row_count), -jnp.inf, jnp.float32),
        jnp.zeros((local_heads, row_count), jnp.float32),
        jnp.zeros((local_heads, row_count, HD), jnp.float32),
    )
    running = initial
    key_piece = lax.all_gather(key_rows, "tp", axis=0, tiled=True)
    value_piece = lax.all_gather(value_rows, "tp", axis=0, tiled=True)
    length = key_piece.shape[0]
    step_rows = key_block if length % key_block == 0 else length
    number = length // step_rows
    key_blocks = key_piece.reshape(number, step_rows, local_heads, HD)
    value_blocks = value_piece.reshape(number, step_rows, local_heads, HD)

    def update(carried, blocks_now):
        highest, totals, summed = carried
        key_now, value_now = blocks_now
        scores = (
            jnp.einsum("qhd,khd->hqk", query_heads, key_now, preferred_element_type=jnp.float32)
            * scaling
        )
        new_highest = jnp.maximum(highest, jnp.max(scores, axis=2))
        fading = jnp.exp(highest - new_highest)
        weights = jnp.exp(scores - new_highest[..., None])
        totals = totals * fading + jnp.sum(weights, axis=2)
        summed = summed * fading[..., None] + jnp.einsum(
            "hqk,khd->hqd",
            weights.astype(jnp.bfloat16),
            value_now,
            preferred_element_type=jnp.float32,
        )
        return ((new_highest, totals, summed), None)

    running, unused = lax.scan(update, running, (key_blocks, value_blocks))
    highest, totals, summed = running
    result = summed / totals[..., None]
    return jnp.transpose(result, (1, 0, 2)).reshape(row_count, columns).astype(jnp.bfloat16)


def by_heads_and_rows(projected, hint_gain, block_map, token_perm):
    block_rows = projected.shape[1]
    features = projected.shape[3]
    seq_count = lax.axis_size("seq")
    tp_count = lax.axis_size("tp")
    branch_index = lax.axis_index("branch")
    seq_index = lax.axis_index("seq")
    tp_index = lax.axis_index("tp")
    arrived = lax.all_to_all(projected[0], "seq", split_axis=2, concat_axis=0, tiled=True)
    columns = features // seq_count
    attended = attend(arrived[:, 0], arrived[:, 1], arrived[:, 2])
    attended = lax.optimization_barrier(attended)
    partner = passed_along(attended, "branch", -1)
    perm_table = token_perm.reshape(seq_count, tp_count, block_rows)
    column = lax.dynamic_index_in_dim(perm_table, tp_index, 1, keepdims=False)
    picked = (block_map[:, None] * block_rows + column).reshape(-1)
    control = jnp.take(partner, picked, axis=0).astype(jnp.float32)
    gain_slice = lax.dynamic_slice_in_dim(hint_gain, seq_index * columns, columns)
    summed = (attended.astype(jnp.float32) + gain_slice * control).astype(jnp.bfloat16)
    result = jnp.where(branch_index == 0, summed, attended)
    return lax.all_to_all(result, "seq", split_axis=0, concat_axis=1, tiled=True)[None]


def on_device(projected, hint_gain, block_map, token_perm):
    count = lax.axis_size("seq") * lax.axis_size("tp")
    rows, heads = projected.shape[1], projected.shape[3] // HD
    if heads % count == 0 and count & (count - 1) == 0 and rows % 16 == 0:
        return by_heads(projected, hint_gain, block_map, token_perm)
    return by_heads_and_rows(projected, hint_gain, block_map, token_perm)


def solution(mesh):
    return jax.shard_map(
        on_device,
        mesh=mesh,
        in_specs=(P("branch", ("req", "seq", "tp"), None, None), P(), P(), P()),
        out_specs=P("branch", ("req", "seq", "tp"), None),
        check_vma=False,
    )
```

```python
import functools
import math

import jax
import jax.numpy as jnp
from jax import lax
from jax.experimental import pallas as pl
from jax.experimental.pallas import tpu as pltpu
from jax.sharding import PartitionSpec as P

HD = 128
VMEM_LIMIT = 32 * 1024 * 1024

key_block = 512

ORDER_IN = ((4, 3, 2, 5, 7, 6, 1), (6, 1, 2, 4, 5, 7, 3))
ORDER_BACK = ((6, 3, 1), (7, 5, 2))
STRAIGHT = (4,)
STRAIGHT_FIRST = False


def group_index():
    return lax.axis_index("seq") * lax.axis_size("tp") + lax.axis_index("tp")


def columns_of(group, step, width):
    return pl.ds(pl.multiple_of(lax.bitwise_xor(group, step) * width, HD), width)


def split_kernel(orders, width, rows_ref, *refs):
    outs, sems = refs[:-1], refs[-1]
    me = group_index()
    copies = []
    for n, steps in enumerate(zip(*orders)):
        step = jnp.where(lax.axis_index("branch") == 0, *steps)
        piece = rows_ref.at[:, :, columns_of(me, step, width)]
        copies.append(pltpu.make_async_copy(piece, outs[n], sems.at[n]))
    for copy in copies:
        copy.start()
    for copy in copies:
        copy.wait()


def attend_kernel(count, rows, start, stop, *refs):
    pieces, out_ref = refs[:count], refs[count]
    scaling = math.log2(math.e) / math.sqrt(HD)
    heads = [slice(first, first + HD) for first in range(start, stop, HD)]
    joined = lambda n, at: jnp.concatenate([piece[n, :, at] for piece in pieces], axis=0)
    scores = [
        lax.dot_general(
            joined(0, at),
            joined(1, at),
            (((1,), (1,)), ((), ())),
            preferred_element_type=jnp.float32,
        )
        for at in heads
    ]
    weighted = []
    for score in scores:
        highest = jnp.max(score, axis=1, keepdims=True)
        weights = jnp.exp2((score - highest) * scaling)
        weighted.append((weights.astype(jnp.bfloat16), jnp.sum(weights, axis=1, keepdims=True)))
    for at, (probs, totals) in zip(heads, weighted):
        summed = jnp.dot(probs, joined(2, at), preferred_element_type=jnp.float32)
        place = slice(at.start - start, at.stop - start)
        out_ref[:, :, place] = (summed / totals).astype(jnp.bfloat16).reshape(count, rows, HD)


def on_branch(work):
    for branch in range(2):
        pl.when(lax.axis_index("branch") == branch)(functools.partial(work, branch))


def choose_kernel(orders_in, orders, rows, map_ref, perm_ref, out_ref):
    on_branch(lambda branch: choose(orders_in[1], orders[branch], rows, map_ref, perm_ref, out_ref))


def choose(order_in, order, rows, map_ref, perm_ref, out_ref):
    me = group_index()
    tp_count = lax.axis_size("tp")
    tokens = len(order) * rows
    lane = lax.broadcasted_iota(jnp.int32, (1, tokens), 1)
    row_of = jnp.zeros((1, tokens), jnp.int32)
    first_of = jnp.zeros((1, tokens), jnp.int32)
    for n, step in enumerate(order):
        block = lax.bitwise_xor(me, step)
        source = map_ref[block // tp_count] * tp_count + block % tp_count
        distance = lax.bitwise_xor(source, me)
        place = sum(jnp.where(distance == far, at, 0) for at, far in enumerate(order_in))
        here = (lane >= n * rows) & (lane < (n + 1) * rows)
        row_of = jnp.where(here, block, row_of)
        first_of = jnp.where(here, place * rows, first_of)
    within = lax.broadcasted_iota(jnp.int32, (rows, tokens), 0)
    repeat = sum((within + n * rows == lane).astype(jnp.float32) for n in range(len(order)))
    perms = jnp.dot(
        perm_ref[...].astype(jnp.float32),
        repeat,
        precision=lax.Precision.HIGHEST,
        preferred_element_type=jnp.float32,
    )
    number = lax.broadcasted_iota(jnp.int32, perms.shape, 0)
    perm = jnp.sum(jnp.where(number == row_of, perms, 0.0), axis=0, keepdims=True)
    source_token = first_of.astype(jnp.float32) + perm
    shape = (len(order_in) * rows, tokens)
    column = lax.broadcasted_iota(jnp.int32, shape, 0).astype(jnp.float32)
    out_ref[...] = (column == source_token).astype(jnp.float32).T.astype(out_ref.dtype)


def join_kernel(orders_in, orders, straight, rows, width, chosen_ref, gain_ref, own_refs, other_refs, *outs):
    def work(branch):
        base_refs, control_refs = (own_refs, other_refs) if branch == 0 else (other_refs, own_refs)
        start = 0
        for base_ref, control_ref in zip(base_refs, control_refs):
            stop = start + base_ref.shape[2]
            at = slice(start, stop)
            gain = gain_ref[:, at]
            hint = jnp.dot(
                chosen_ref[...],
                control_ref[...].reshape(len(orders_in[1]) * rows, stop - start),
                preferred_element_type=jnp.float32,
            )
            for n, step in enumerate(orders[branch] + straight + [0]):
                control = control_ref[orders_in[1].index(step)]
                base = base_ref[orders_in[0].index(step)].astype(jnp.float32)
                added = gain * hint[n * rows : (n + 1) * rows]
                joined = (base + added).astype(jnp.bfloat16)
                if n < len(orders[branch]):
                    outs[n][branch, :, at] = joined
                    outs[n][1 - branch, :, at] = control
                else:
                    outs[n][:, at] = joined if branch == 0 else control
            start = stop

    on_branch(work)


def take_kernel(in_ref, out_ref):
    out_ref[...] = in_ref[1]


def merge_kernel(orders, straight, width, *refs):
    out_ref, sems = refs[-2:]
    if STRAIGHT_FIRST:
        own_refs, pair_refs, passed_refs = refs[:-2]
    else:
        pair_refs, passed_refs, own_refs = refs[:-2]

    def work(branch):
        me = group_index()
        pieces = [(ref.at[0], step) for ref, step in zip(pair_refs, orders[branch])]
        pieces += zip(passed_refs, orders[1 - branch])
        pieces += zip(own_refs, straight + [0])
        copies = []
        for n, (piece, step) in enumerate(pieces):
            place = out_ref.at[:, columns_of(me, step, width)]
            copies.append(pltpu.make_async_copy(piece, place, sems.at[n]))
        for copy in copies:
            copy.start()
        for copy in copies:
            copy.wait()

    on_branch(work)


def any_specs(number):
    return [pl.BlockSpec(memory_space=pl.ANY)] * number


def vmem_specs(number):
    return [pl.BlockSpec(memory_space=pltpu.VMEM)] * number


PARAMS = pltpu.CompilerParams(vmem_limit_bytes=VMEM_LIMIT)


def in_order(order, count):
    first = [step for step in order if step < count]
    return first + [step for step in range(1, count) if step not in first] + [0]


def back_plan(count):
    orders, straight = [list(order) for order in ORDER_BACK], list(STRAIGHT)
    steps = list(range(1, count))
    if sorted(orders[0] + orders[1] + straight) != steps:
        half = len(steps) // 2
        orders, straight = [steps[:half], steps[half : 2 * half]], steps[2 * half :]
    return orders, straight


def exchange_by_core(pieces, orders):
    tp_count = lax.axis_size("tp")
    groups = range(lax.axis_size("seq") * tp_count)
    device = lambda group, core: (group // tp_count * 2 + core) * tp_count + group % tp_count
    arrived = []
    for piece, steps in zip(pieces, zip(*orders)):
        pairs = [(device(g, core), device(g ^ steps[core], core)) for g in groups for core in (0, 1)]
        moved = any(steps)
        arrived.append(lax.ppermute(piece, ("seq", "branch", "tp"), pairs) if moved else piece)
    return arrived


def by_heads(projected, hint_gain, block_map, token_perm):
    rows, features = projected.shape[1], projected.shape[3]
    count = lax.axis_size("seq") * lax.axis_size("tp")
    width = features // count
    orders_in = [in_order(order, count) for order in ORDER_IN]
    orders_back, straight = back_plan(count)
    pairs = len(orders_back[0])
    stays = len(straight) + 1
    middle = width // HD // 2 * HD
    parts = [(0, width)]
    dtype = projected.dtype
    both = [(0, 1), (1, 0)]
    sent = pl.pallas_call(
        functools.partial(split_kernel, orders_in, width),
        out_shape=[jax.ShapeDtypeStruct((3, rows, width), dtype)] * count,
        in_specs=any_specs(1),
        out_specs=any_specs(count),
        scratch_shapes=[pltpu.SemaphoreType.DMA((count,))],
        compiler_params=PARAMS,
        name="split",
    )(jnp.transpose(projected[0], (1, 0, 2)))
    arrived = exchange_by_core(sent, orders_in)
    attended = [
        pl.pallas_call(
            functools.partial(attend_kernel, count, rows, start, stop),
            out_shape=jax.ShapeDtypeStruct((count, rows, stop - start), dtype),
            in_specs=vmem_specs(count),
            out_specs=vmem_specs(1)[0],
            compiler_params=PARAMS,
            name="attend",
        )(*arrived)
        for start, stop in parts
    ]
    other = [lax.ppermute(part, "branch", both) for part in attended]
    block_map, attended[-1] = lax.optimization_barrier((block_map, attended[-1]))
    chosen = pl.pallas_call(
        functools.partial(choose_kernel, orders_in, [order + straight + [0] for order in orders_back], rows),
        out_shape=jax.ShapeDtypeStruct(((pairs + stays) * rows, count * rows), dtype),
        in_specs=[pl.BlockSpec(memory_space=pltpu.SMEM)] + vmem_specs(1),
        out_specs=vmem_specs(1)[0],
        compiler_params=PARAMS,
        name="choose",
    )(block_map, token_perm)
    gain = lax.dynamic_slice_in_dim(hint_gain, group_index() * width, width)[None, :]
    joined = pl.pallas_call(
        functools.partial(join_kernel, orders_in, orders_back, straight, rows, width),
        out_shape=[jax.ShapeDtypeStruct((2, rows, width), dtype)] * pairs
        + [jax.ShapeDtypeStruct((rows, width), dtype)] * stays,
        in_specs=vmem_specs(2) + [vmem_specs(len(parts))] * 2,
        out_specs=vmem_specs(pairs + stays),
        compiler_params=PARAMS,
        name="join",
    )(chosen, gain, attended, other)
    returned = exchange_by_core(joined, [order + straight + [0] for order in orders_back])
    passed = []
    for piece in returned[:pairs]:
        taken = pl.pallas_call(
            take_kernel,
            out_shape=jax.ShapeDtypeStruct((rows, width), dtype),
            in_specs=vmem_specs(1),
            out_specs=vmem_specs(1)[0],
            compiler_params=PARAMS,
            name="take",
        )(piece)
        passed.append(lax.ppermute(taken, "branch", both))
    groups = [returned[:pairs], passed]
    groups.insert(0 if STRAIGHT_FIRST else 2, returned[pairs:])
    result = pl.pallas_call(
        functools.partial(merge_kernel, orders_back, straight, width),
        out_shape=jax.ShapeDtypeStruct((rows, features), dtype),
        in_specs=[any_specs(len(group)) for group in groups],
        out_specs=any_specs(1)[0],
        scratch_shapes=[pltpu.SemaphoreType.DMA((count,))],
        compiler_params=PARAMS,
        name="merge",
    )(*groups)
    return result[None]


def passed_along(x, axis, by):
    count = lax.axis_size(axis)
    pairs = [(i, i + by) for i in range(count) if 0 <= i + by < count]
    return lax.ppermute(x, axis, pairs)


def attend(queries, key_rows, value_rows):
    row_count, columns = queries.shape
    local_heads = columns // HD
    query_heads = queries.reshape(row_count, local_heads, HD)
    scaling = 1.0 / math.sqrt(HD)
    initial = (
        jnp.full((local_heads, row_count), -jnp.inf, jnp.float32),
        jnp.zeros((local_heads, row_count), jnp.float32),
        jnp.zeros((local_heads, row_count, HD), jnp.float32),
    )
    running = initial
    key_piece = lax.all_gather(key_rows, "tp", axis=0, tiled=True)
    value_piece = lax.all_gather(value_rows, "tp", axis=0, tiled=True)
    length = key_piece.shape[0]
    step_rows = key_block if length % key_block == 0 else length
    number = length // step_rows
    key_blocks = key_piece.reshape(number, step_rows, local_heads, HD)
    value_blocks = value_piece.reshape(number, step_rows, local_heads, HD)

    def update(carried, blocks_now):
        highest, totals, summed = carried
        key_now, value_now = blocks_now
        scores = (
            jnp.einsum("qhd,khd->hqk", query_heads, key_now, preferred_element_type=jnp.float32)
            * scaling
        )
        new_highest = jnp.maximum(highest, jnp.max(scores, axis=2))
        fading = jnp.exp(highest - new_highest)
        weights = jnp.exp(scores - new_highest[..., None])
        totals = totals * fading + jnp.sum(weights, axis=2)
        summed = summed * fading[..., None] + jnp.einsum(
            "hqk,khd->hqd",
            weights.astype(jnp.bfloat16),
            value_now,
            preferred_element_type=jnp.float32,
        )
        return ((new_highest, totals, summed), None)

    running, unused = lax.scan(update, running, (key_blocks, value_blocks))
    highest, totals, summed = running
    result = summed / totals[..., None]
    return jnp.transpose(result, (1, 0, 2)).reshape(row_count, columns).astype(jnp.bfloat16)


def by_heads_and_rows(projected, hint_gain, block_map, token_perm):
    block_rows = projected.shape[1]
    features = projected.shape[3]
    seq_count = lax.axis_size("seq")
    tp_count = lax.axis_size("tp")
    branch_index = lax.axis_index("branch")
    seq_index = lax.axis_index("seq")
    tp_index = lax.axis_index("tp")
    arrived = lax.all_to_all(projected[0], "seq", split_axis=2, concat_axis=0, tiled=True)
    columns = features // seq_count
    attended = attend(arrived[:, 0], arrived[:, 1], arrived[:, 2])
    attended = lax.optimization_barrier(attended)
    partner = passed_along(attended, "branch", -1)
    perm_table = token_perm.reshape(seq_count, tp_count, block_rows)
    column = lax.dynamic_index_in_dim(perm_table, tp_index, 1, keepdims=False)
    picked = (block_map[:, None] * block_rows + column).reshape(-1)
    control = jnp.take(partner, picked, axis=0).astype(jnp.float32)
    gain_slice = lax.dynamic_slice_in_dim(hint_gain, seq_index * columns, columns)
    summed = (attended.astype(jnp.float32) + gain_slice * control).astype(jnp.bfloat16)
    result = jnp.where(branch_index == 0, summed, attended)
    return lax.all_to_all(result, "seq", split_axis=0, concat_axis=1, tiled=True)[None]


def on_device(projected, hint_gain, block_map, token_perm):
    count = lax.axis_size("seq") * lax.axis_size("tp")
    rows, heads = projected.shape[1], projected.shape[3] // HD
    if heads % count == 0 and count & (count - 1) == 0 and rows % 16 == 0:
        return by_heads(projected, hint_gain, block_map, token_perm)
    return by_heads_and_rows(projected, hint_gain, block_map, token_perm)


def solution(mesh):
    return jax.shard_map(
        on_device,
        mesh=mesh,
        in_specs=(P("branch", ("req", "seq", "tp"), None, None), P(), P(), P()),
        out_specs=P("branch", ("req", "seq", "tp"), None),
        check_vma=False,
    )
```

```python
import functools
import math

import jax
import jax.numpy as jnp
from jax import lax
from jax.experimental import pallas as pl
from jax.experimental.pallas import tpu as pltpu
from jax.sharding import PartitionSpec as P

HD = 128
VMEM_LIMIT = 32 * 1024 * 1024

key_block = 512

ORDER_IN = ((4, 3, 2, 5, 7, 6, 1), (6, 1, 2, 4, 5, 7, 3))
ORDER_BACK = ((6, 3, 1), (7, 5, 2))
STRAIGHT = (4,)
STRAIGHT_FIRST = False


def group_index():
    return lax.axis_index("seq") * lax.axis_size("tp") + lax.axis_index("tp")


def columns_of(group, step, width):
    return pl.ds(pl.multiple_of(lax.bitwise_xor(group, step) * width, HD), width)


def split_kernel(orders, width, rows_ref, *refs):
    outs, sems = refs[:-1], refs[-1]
    me = group_index()
    copies = []
    for n, steps in enumerate(zip(*orders)):
        step = jnp.where(lax.axis_index("branch") == 0, *steps)
        piece = rows_ref.at[:, :, columns_of(me, step, width)]
        copies.append(pltpu.make_async_copy(piece, outs[n], sems.at[n]))
    for copy in copies:
        copy.start()
    for copy in copies:
        copy.wait()


def attend_kernel(count, rows, start, stop, *refs):
    pieces, out_ref = refs[:count], refs[count]
    scaling = math.log2(math.e) / math.sqrt(HD)
    heads = [slice(first, first + HD) for first in range(start, stop, HD)]
    joined = lambda n, at: jnp.concatenate([piece[n, :, at] for piece in pieces], axis=0)
    scores = [
        lax.dot_general(
            joined(0, at),
            joined(1, at),
            (((1,), (1,)), ((), ())),
            preferred_element_type=jnp.float32,
        )
        for at in heads
    ]
    weighted = []
    for score in scores:
        highest = jnp.max(score, axis=1, keepdims=True)
        weights = jnp.exp2((score - highest) * scaling)
        weighted.append((weights.astype(jnp.bfloat16), jnp.sum(weights, axis=1, keepdims=True)))
    for at, (probs, totals) in zip(heads, weighted):
        summed = jnp.dot(probs, joined(2, at), preferred_element_type=jnp.float32)
        place = slice(at.start - start, at.stop - start)
        out_ref[:, :, place] = (summed / totals).astype(jnp.bfloat16).reshape(count, rows, HD)


def on_branch(work):
    for branch in range(2):
        pl.when(lax.axis_index("branch") == branch)(functools.partial(work, branch))


def choose_kernel(orders_in, orders, rows, map_ref, perm_ref, out_ref):
    on_branch(lambda branch: choose(orders_in[1], orders[branch], rows, map_ref, perm_ref, out_ref))


def choose(order_in, order, rows, map_ref, perm_ref, out_ref):
    me = group_index()
    tp_count = lax.axis_size("tp")
    tokens = len(order) * rows
    lane = lax.broadcasted_iota(jnp.int32, (1, tokens), 1)
    row_of = jnp.zeros((1, tokens), jnp.int32)
    first_of = jnp.zeros((1, tokens), jnp.int32)
    for n, step in enumerate(order):
        block = lax.bitwise_xor(me, step)
        source = map_ref[block // tp_count] * tp_count + block % tp_count
        distance = lax.bitwise_xor(source, me)
        place = sum(jnp.where(distance == far, at, 0) for at, far in enumerate(order_in))
        here = (lane >= n * rows) & (lane < (n + 1) * rows)
        row_of = jnp.where(here, block, row_of)
        first_of = jnp.where(here, place * rows, first_of)
    within = lax.broadcasted_iota(jnp.int32, (rows, tokens), 0)
    repeat = sum((within + n * rows == lane).astype(jnp.float32) for n in range(len(order)))
    perms = jnp.dot(
        perm_ref[...].astype(jnp.float32),
        repeat,
        precision=lax.Precision.HIGHEST,
        preferred_element_type=jnp.float32,
    )
    number = lax.broadcasted_iota(jnp.int32, perms.shape, 0)
    perm = jnp.sum(jnp.where(number == row_of, perms, 0.0), axis=0, keepdims=True)
    source_token = first_of.astype(jnp.float32) + perm
    shape = (len(order_in) * rows, tokens)
    column = lax.broadcasted_iota(jnp.int32, shape, 0).astype(jnp.float32)
    out_ref[...] = (column == source_token).astype(jnp.float32).T.astype(out_ref.dtype)


def join_kernel(orders_in, orders, straight, rows, width, chosen_ref, gain_ref, own_refs, other_refs, *outs):
    def work(branch):
        base_refs, control_refs = (own_refs, other_refs) if branch == 0 else (other_refs, own_refs)
        start = 0
        for base_ref, control_ref in zip(base_refs, control_refs):
            stop = start + base_ref.shape[2]
            at = slice(start, stop)
            first = pl.multiple_of(group_index() * width + start, HD)
            gain = gain_ref[:, pl.ds(first, stop - start)]
            hint = jnp.dot(
                chosen_ref[...],
                control_ref[...].reshape(len(orders_in[1]) * rows, stop - start),
                preferred_element_type=jnp.float32,
            )
            for n, step in enumerate(orders[branch] + straight + [0]):
                control = control_ref[orders_in[1].index(step)]
                base = base_ref[orders_in[0].index(step)].astype(jnp.float32)
                added = gain * hint[n * rows : (n + 1) * rows]
                joined = (base + added).astype(jnp.bfloat16)
                if n < len(orders[branch]):
                    outs[n][branch, :, at] = joined
                    outs[n][1 - branch, :, at] = control
                else:
                    outs[n][:, at] = joined if branch == 0 else control
            start = stop

    on_branch(work)


def take_kernel(in_ref, out_ref):
    out_ref[...] = in_ref[1]


def merge_kernel(orders, straight, width, *refs):
    out_ref, sems = refs[-2:]
    if STRAIGHT_FIRST:
        own_refs, pair_refs, passed_refs = refs[:-2]
    else:
        pair_refs, passed_refs, own_refs = refs[:-2]

    def work(branch):
        me = group_index()
        pieces = [(ref.at[0], step) for ref, step in zip(pair_refs, orders[branch])]
        pieces += zip(passed_refs, orders[1 - branch])
        pieces += zip(own_refs, straight + [0])
        copies = []
        for n, (piece, step) in enumerate(pieces):
            place = out_ref.at[:, columns_of(me, step, width)]
            copies.append(pltpu.make_async_copy(piece, place, sems.at[n]))
        for copy in copies:
            copy.start()
        for copy in copies:
            copy.wait()

    on_branch(work)


def any_specs(number):
    return [pl.BlockSpec(memory_space=pl.ANY)] * number


def vmem_specs(number):
    return [pl.BlockSpec(memory_space=pltpu.VMEM)] * number


PARAMS = pltpu.CompilerParams(vmem_limit_bytes=VMEM_LIMIT)


def in_order(order, count):
    first = [step for step in order if step < count]
    return first + [step for step in range(1, count) if step not in first] + [0]


def back_plan(count):
    orders, straight = [list(order) for order in ORDER_BACK], list(STRAIGHT)
    steps = list(range(1, count))
    if sorted(orders[0] + orders[1] + straight) != steps:
        half = len(steps) // 2
        orders, straight = [steps[:half], steps[half : 2 * half]], steps[2 * half :]
    return orders, straight


def exchange_by_core(pieces, orders):
    tp_count = lax.axis_size("tp")
    groups = range(lax.axis_size("seq") * tp_count)
    device = lambda group, core: (group // tp_count * 2 + core) * tp_count + group % tp_count
    arrived = []
    for piece, steps in zip(pieces, zip(*orders)):
        pairs = [(device(g, core), device(g ^ steps[core], core)) for g in groups for core in (0, 1)]
        moved = any(steps)
        arrived.append(lax.ppermute(piece, ("seq", "branch", "tp"), pairs) if moved else piece)
    return arrived


def by_heads(projected, hint_gain, block_map, token_perm):
    rows, features = projected.shape[1], projected.shape[3]
    count = lax.axis_size("seq") * lax.axis_size("tp")
    width = features // count
    orders_in = [in_order(order, count) for order in ORDER_IN]
    orders_back, straight = back_plan(count)
    pairs = len(orders_back[0])
    stays = len(straight) + 1
    middle = width // HD // 2 * HD
    parts = [(0, width)]
    dtype = projected.dtype
    both = [(0, 1), (1, 0)]
    sent = pl.pallas_call(
        functools.partial(split_kernel, orders_in, width),
        out_shape=[jax.ShapeDtypeStruct((3, rows, width), dtype)] * count,
        in_specs=any_specs(1),
        out_specs=any_specs(count),
        scratch_shapes=[pltpu.SemaphoreType.DMA((count,))],
        compiler_params=PARAMS,
        name="split",
    )(jnp.transpose(projected[0], (1, 0, 2)))
    arrived = exchange_by_core(sent, orders_in)
    attended = [
        pl.pallas_call(
            functools.partial(attend_kernel, count, rows, start, stop),
            out_shape=jax.ShapeDtypeStruct((count, rows, stop - start), dtype),
            in_specs=vmem_specs(count),
            out_specs=vmem_specs(1)[0],
            compiler_params=PARAMS,
            name="attend",
        )(*arrived)
        for start, stop in parts
    ]
    other = [lax.ppermute(part, "branch", both) for part in attended]
    block_map, attended[-1] = lax.optimization_barrier((block_map, attended[-1]))
    chosen = pl.pallas_call(
        functools.partial(choose_kernel, orders_in, [order + straight + [0] for order in orders_back], rows),
        out_shape=jax.ShapeDtypeStruct(((pairs + stays) * rows, count * rows), dtype),
        in_specs=[pl.BlockSpec(memory_space=pltpu.SMEM)] + vmem_specs(1),
        out_specs=vmem_specs(1)[0],
        compiler_params=PARAMS,
        name="choose",
    )(block_map, token_perm)
    joined = pl.pallas_call(
        functools.partial(join_kernel, orders_in, orders_back, straight, rows, width),
        out_shape=[jax.ShapeDtypeStruct((2, rows, width), dtype)] * pairs
        + [jax.ShapeDtypeStruct((rows, width), dtype)] * stays,
        in_specs=vmem_specs(2) + [vmem_specs(len(parts))] * 2,
        out_specs=vmem_specs(pairs + stays),
        compiler_params=PARAMS,
        name="join",
    )(chosen, hint_gain[None, :], attended, other)
    returned = exchange_by_core(joined, [order + straight + [0] for order in orders_back])
    passed = []
    for piece in returned[:pairs]:
        taken = pl.pallas_call(
            take_kernel,
            out_shape=jax.ShapeDtypeStruct((rows, width), dtype),
            in_specs=vmem_specs(1),
            out_specs=vmem_specs(1)[0],
            compiler_params=PARAMS,
            name="take",
        )(piece)
        passed.append(lax.ppermute(taken, "branch", both))
    groups = [returned[:pairs], passed]
    groups.insert(0 if STRAIGHT_FIRST else 2, returned[pairs:])
    result = pl.pallas_call(
        functools.partial(merge_kernel, orders_back, straight, width),
        out_shape=jax.ShapeDtypeStruct((rows, features), dtype),
        in_specs=[any_specs(len(group)) for group in groups],
        out_specs=any_specs(1)[0],
        scratch_shapes=[pltpu.SemaphoreType.DMA((count,))],
        compiler_params=PARAMS,
        name="merge",
    )(*groups)
    return result[None]


def passed_along(x, axis, by):
    count = lax.axis_size(axis)
    pairs = [(i, i + by) for i in range(count) if 0 <= i + by < count]
    return lax.ppermute(x, axis, pairs)


def attend(queries, key_rows, value_rows):
    row_count, columns = queries.shape
    local_heads = columns // HD
    query_heads = queries.reshape(row_count, local_heads, HD)
    scaling = 1.0 / math.sqrt(HD)
    initial = (
        jnp.full((local_heads, row_count), -jnp.inf, jnp.float32),
        jnp.zeros((local_heads, row_count), jnp.float32),
        jnp.zeros((local_heads, row_count, HD), jnp.float32),
    )
    running = initial
    key_piece = lax.all_gather(key_rows, "tp", axis=0, tiled=True)
    value_piece = lax.all_gather(value_rows, "tp", axis=0, tiled=True)
    length = key_piece.shape[0]
    step_rows = key_block if length % key_block == 0 else length
    number = length // step_rows
    key_blocks = key_piece.reshape(number, step_rows, local_heads, HD)
    value_blocks = value_piece.reshape(number, step_rows, local_heads, HD)

    def update(carried, blocks_now):
        highest, totals, summed = carried
        key_now, value_now = blocks_now
        scores = (
            jnp.einsum("qhd,khd->hqk", query_heads, key_now, preferred_element_type=jnp.float32)
            * scaling
        )
        new_highest = jnp.maximum(highest, jnp.max(scores, axis=2))
        fading = jnp.exp(highest - new_highest)
        weights = jnp.exp(scores - new_highest[..., None])
        totals = totals * fading + jnp.sum(weights, axis=2)
        summed = summed * fading[..., None] + jnp.einsum(
            "hqk,khd->hqd",
            weights.astype(jnp.bfloat16),
            value_now,
            preferred_element_type=jnp.float32,
        )
        return ((new_highest, totals, summed), None)

    running, unused = lax.scan(update, running, (key_blocks, value_blocks))
    highest, totals, summed = running
    result = summed / totals[..., None]
    return jnp.transpose(result, (1, 0, 2)).reshape(row_count, columns).astype(jnp.bfloat16)


def by_heads_and_rows(projected, hint_gain, block_map, token_perm):
    block_rows = projected.shape[1]
    features = projected.shape[3]
    seq_count = lax.axis_size("seq")
    tp_count = lax.axis_size("tp")
    branch_index = lax.axis_index("branch")
    seq_index = lax.axis_index("seq")
    tp_index = lax.axis_index("tp")
    arrived = lax.all_to_all(projected[0], "seq", split_axis=2, concat_axis=0, tiled=True)
    columns = features // seq_count
    attended = attend(arrived[:, 0], arrived[:, 1], arrived[:, 2])
    attended = lax.optimization_barrier(attended)
    partner = passed_along(attended, "branch", -1)
    perm_table = token_perm.reshape(seq_count, tp_count, block_rows)
    column = lax.dynamic_index_in_dim(perm_table, tp_index, 1, keepdims=False)
    picked = (block_map[:, None] * block_rows + column).reshape(-1)
    control = jnp.take(partner, picked, axis=0).astype(jnp.float32)
    gain_slice = lax.dynamic_slice_in_dim(hint_gain, seq_index * columns, columns)
    summed = (attended.astype(jnp.float32) + gain_slice * control).astype(jnp.bfloat16)
    result = jnp.where(branch_index == 0, summed, attended)
    return lax.all_to_all(result, "seq", split_axis=0, concat_axis=1, tiled=True)[None]


def on_device(projected, hint_gain, block_map, token_perm):
    count = lax.axis_size("seq") * lax.axis_size("tp")
    rows, heads = projected.shape[1], projected.shape[3] // HD
    if heads % count == 0 and count & (count - 1) == 0 and rows % 16 == 0:
        return by_heads(projected, hint_gain, block_map, token_perm)
    return by_heads_and_rows(projected, hint_gain, block_map, token_perm)


def solution(mesh):
    return jax.shard_map(
        on_device,
        mesh=mesh,
        in_specs=(P("branch", ("req", "seq", "tp"), None, None), P(), P(), P()),
        out_specs=P("branch", ("req", "seq", "tp"), None),
        check_vma=False,
    )
```

```python
import functools
import math

import jax
import jax.numpy as jnp
from jax import lax
from jax.experimental import pallas as pl
from jax.experimental.pallas import tpu as pltpu
from jax.sharding import PartitionSpec as P

HD = 128
VMEM_LIMIT = 32 * 1024 * 1024

key_block = 512

ORDER_IN = ((4, 3, 2, 5, 7, 6, 1), (6, 2, 1, 4, 5, 7, 3))
ORDER_BACK = ((6, 3, 1), (7, 5, 2))
STRAIGHT = (4,)
STRAIGHT_FIRST = False


def group_index():
    return lax.axis_index("seq") * lax.axis_size("tp") + lax.axis_index("tp")


def columns_of(group, step, width):
    return pl.ds(pl.multiple_of(lax.bitwise_xor(group, step) * width, HD), width)


def split_kernel(orders, width, rows_ref, *refs):
    outs, sems = refs[:-1], refs[-1]
    me = group_index()
    copies = []
    for n, steps in enumerate(zip(*orders)):
        step = jnp.where(lax.axis_index("branch") == 0, *steps)
        piece = rows_ref.at[:, :, columns_of(me, step, width)]
        copies.append(pltpu.make_async_copy(piece, outs[n], sems.at[n]))
    for copy in copies:
        copy.start()
    for copy in copies:
        copy.wait()


def attend_kernel(count, rows, start, stop, *refs):
    pieces, out_ref = refs[:count], refs[count]
    scaling = math.log2(math.e) / math.sqrt(HD)
    heads = [slice(first, first + HD) for first in range(start, stop, HD)]
    joined = lambda n, at: jnp.concatenate([piece[n, :, at] for piece in pieces], axis=0)
    scores = [
        lax.dot_general(
            joined(0, at),
            joined(1, at),
            (((1,), (1,)), ((), ())),
            preferred_element_type=jnp.float32,
        )
        for at in heads
    ]
    weighted = []
    for score in scores:
        highest = jnp.max(score, axis=1, keepdims=True)
        weights = jnp.exp2((score - highest) * scaling)
        weighted.append((weights.astype(jnp.bfloat16), jnp.sum(weights, axis=1, keepdims=True)))
    for at, (probs, totals) in zip(heads, weighted):
        summed = jnp.dot(probs, joined(2, at), preferred_element_type=jnp.float32)
        place = slice(at.start - start, at.stop - start)
        out_ref[:, :, place] = (summed / totals).astype(jnp.bfloat16).reshape(count, rows, HD)


def on_branch(work):
    for branch in range(2):
        pl.when(lax.axis_index("branch") == branch)(functools.partial(work, branch))


def choose_kernel(orders_in, orders, rows, map_ref, perm_ref, out_ref):
    on_branch(lambda branch: choose(orders_in[1], orders[branch], rows, map_ref, perm_ref, out_ref))


def choose(order_in, order, rows, map_ref, perm_ref, out_ref):
    me = group_index()
    tp_count = lax.axis_size("tp")
    tokens = len(order) * rows
    lane = lax.broadcasted_iota(jnp.int32, (1, tokens), 1)
    row_of = jnp.zeros((1, tokens), jnp.int32)
    first_of = jnp.zeros((1, tokens), jnp.int32)
    for n, step in enumerate(order):
        block = lax.bitwise_xor(me, step)
        source = map_ref[block // tp_count] * tp_count + block % tp_count
        distance = lax.bitwise_xor(source, me)
        place = sum(jnp.where(distance == far, at, 0) for at, far in enumerate(order_in))
        here = (lane >= n * rows) & (lane < (n + 1) * rows)
        row_of = jnp.where(here, block, row_of)
        first_of = jnp.where(here, place * rows, first_of)
    within = lax.broadcasted_iota(jnp.int32, (rows, tokens), 0)
    repeat = sum((within + n * rows == lane).astype(jnp.float32) for n in range(len(order)))
    perms = jnp.dot(
        perm_ref[...].astype(jnp.float32),
        repeat,
        precision=lax.Precision.HIGHEST,
        preferred_element_type=jnp.float32,
    )
    number = lax.broadcasted_iota(jnp.int32, perms.shape, 0)
    perm = jnp.sum(jnp.where(number == row_of, perms, 0.0), axis=0, keepdims=True)
    source_token = first_of.astype(jnp.float32) + perm
    shape = (len(order_in) * rows, tokens)
    column = lax.broadcasted_iota(jnp.int32, shape, 0).astype(jnp.float32)
    out_ref[...] = (column == source_token).astype(jnp.float32).T.astype(out_ref.dtype)


def join_kernel(orders_in, orders, straight, rows, width, chosen_ref, gain_ref, own_refs, other_refs, *outs):
    def work(branch):
        base_refs, control_refs = (own_refs, other_refs) if branch == 0 else (other_refs, own_refs)
        start = 0
        for base_ref, control_ref in zip(base_refs, control_refs):
            stop = start + base_ref.shape[2]
            at = slice(start, stop)
            first = pl.multiple_of(group_index() * width + start, HD)
            gain = gain_ref[:, pl.ds(first, stop - start)]
            hint = jnp.dot(
                chosen_ref[...],
                control_ref[...].reshape(len(orders_in[1]) * rows, stop - start),
                preferred_element_type=jnp.float32,
            )
            for n, step in enumerate(orders[branch] + straight + [0]):
                control = control_ref[orders_in[1].index(step)]
                base = base_ref[orders_in[0].index(step)].astype(jnp.float32)
                added = gain * hint[n * rows : (n + 1) * rows]
                joined = (base + added).astype(jnp.bfloat16)
                if n < len(orders[branch]):
                    outs[n][branch, :, at] = joined
                    outs[n][1 - branch, :, at] = control
                else:
                    outs[n][:, at] = joined if branch == 0 else control
            start = stop

    on_branch(work)


def take_kernel(in_ref, out_ref):
    out_ref[...] = in_ref[1]


def merge_kernel(orders, straight, width, *refs):
    out_ref, sems = refs[-2:]
    if STRAIGHT_FIRST:
        own_refs, pair_refs, passed_refs = refs[:-2]
    else:
        pair_refs, passed_refs, own_refs = refs[:-2]

    def work(branch):
        me = group_index()
        pieces = [(ref.at[0], step) for ref, step in zip(pair_refs, orders[branch])]
        pieces += zip(passed_refs, orders[1 - branch])
        pieces += zip(own_refs, straight + [0])
        copies = []
        for n, (piece, step) in enumerate(pieces):
            place = out_ref.at[:, columns_of(me, step, width)]
            copies.append(pltpu.make_async_copy(piece, place, sems.at[n]))
        for copy in copies:
            copy.start()
        for copy in copies:
            copy.wait()

    on_branch(work)


def any_specs(number):
    return [pl.BlockSpec(memory_space=pl.ANY)] * number


def vmem_specs(number):
    return [pl.BlockSpec(memory_space=pltpu.VMEM)] * number


PARAMS = pltpu.CompilerParams(vmem_limit_bytes=VMEM_LIMIT)


def in_order(order, count):
    first = [step for step in order if step < count]
    return first + [step for step in range(1, count) if step not in first] + [0]


def back_plan(count):
    orders, straight = [list(order) for order in ORDER_BACK], list(STRAIGHT)
    steps = list(range(1, count))
    if sorted(orders[0] + orders[1] + straight) != steps:
        half = len(steps) // 2
        orders, straight = [steps[:half], steps[half : 2 * half]], steps[2 * half :]
    return orders, straight


def exchange_by_core(pieces, orders):
    tp_count = lax.axis_size("tp")
    groups = range(lax.axis_size("seq") * tp_count)
    device = lambda group, core: (group // tp_count * 2 + core) * tp_count + group % tp_count
    arrived = []
    for piece, steps in zip(pieces, zip(*orders)):
        pairs = [(device(g, core), device(g ^ steps[core], core)) for g in groups for core in (0, 1)]
        moved = any(steps)
        arrived.append(lax.ppermute(piece, ("seq", "branch", "tp"), pairs) if moved else piece)
    return arrived


def by_heads(projected, hint_gain, block_map, token_perm):
    rows, features = projected.shape[1], projected.shape[3]
    count = lax.axis_size("seq") * lax.axis_size("tp")
    width = features // count
    orders_in = [in_order(order, count) for order in ORDER_IN]
    orders_back, straight = back_plan(count)
    pairs = len(orders_back[0])
    stays = len(straight) + 1
    middle = width // HD // 2 * HD
    parts = [(0, width)]
    dtype = projected.dtype
    both = [(0, 1), (1, 0)]
    sent = pl.pallas_call(
        functools.partial(split_kernel, orders_in, width),
        out_shape=[jax.ShapeDtypeStruct((3, rows, width), dtype)] * count,
        in_specs=any_specs(1),
        out_specs=any_specs(count),
        scratch_shapes=[pltpu.SemaphoreType.DMA((count,))],
        compiler_params=PARAMS,
        name="split",
    )(jnp.transpose(projected[0], (1, 0, 2)))
    arrived = exchange_by_core(sent, orders_in)
    attended = [
        pl.pallas_call(
            functools.partial(attend_kernel, count, rows, start, stop),
            out_shape=jax.ShapeDtypeStruct((count, rows, stop - start), dtype),
            in_specs=vmem_specs(count),
            out_specs=vmem_specs(1)[0],
            compiler_params=PARAMS,
            name="attend",
        )(*arrived)
        for start, stop in parts
    ]
    other = [lax.ppermute(part, "branch", both) for part in attended]
    block_map, attended[-1] = lax.optimization_barrier((block_map, attended[-1]))
    chosen = pl.pallas_call(
        functools.partial(choose_kernel, orders_in, [order + straight + [0] for order in orders_back], rows),
        out_shape=jax.ShapeDtypeStruct(((pairs + stays) * rows, count * rows), dtype),
        in_specs=[pl.BlockSpec(memory_space=pltpu.SMEM)] + vmem_specs(1),
        out_specs=vmem_specs(1)[0],
        compiler_params=PARAMS,
        name="choose",
    )(block_map, token_perm)
    joined = pl.pallas_call(
        functools.partial(join_kernel, orders_in, orders_back, straight, rows, width),
        out_shape=[jax.ShapeDtypeStruct((2, rows, width), dtype)] * pairs
        + [jax.ShapeDtypeStruct((rows, width), dtype)] * stays,
        in_specs=vmem_specs(2) + [vmem_specs(len(parts))] * 2,
        out_specs=vmem_specs(pairs + stays),
        compiler_params=PARAMS,
        name="join",
    )(chosen, hint_gain[None, :], attended, other)
    returned = exchange_by_core(joined, [order + straight + [0] for order in orders_back])
    passed = []
    for piece in returned[:pairs]:
        taken = pl.pallas_call(
            take_kernel,
            out_shape=jax.ShapeDtypeStruct((rows, width), dtype),
            in_specs=vmem_specs(1),
            out_specs=vmem_specs(1)[0],
            compiler_params=PARAMS,
            name="take",
        )(piece)
        passed.append(lax.ppermute(taken, "branch", both))
    groups = [returned[:pairs], passed]
    groups.insert(0 if STRAIGHT_FIRST else 2, returned[pairs:])
    result = pl.pallas_call(
        functools.partial(merge_kernel, orders_back, straight, width),
        out_shape=jax.ShapeDtypeStruct((rows, features), dtype),
        in_specs=[any_specs(len(group)) for group in groups],
        out_specs=any_specs(1)[0],
        scratch_shapes=[pltpu.SemaphoreType.DMA((count,))],
        compiler_params=PARAMS,
        name="merge",
    )(*groups)
    return result[None]


def passed_along(x, axis, by):
    count = lax.axis_size(axis)
    pairs = [(i, i + by) for i in range(count) if 0 <= i + by < count]
    return lax.ppermute(x, axis, pairs)


def attend(queries, key_rows, value_rows):
    row_count, columns = queries.shape
    local_heads = columns // HD
    query_heads = queries.reshape(row_count, local_heads, HD)
    scaling = 1.0 / math.sqrt(HD)
    initial = (
        jnp.full((local_heads, row_count), -jnp.inf, jnp.float32),
        jnp.zeros((local_heads, row_count), jnp.float32),
        jnp.zeros((local_heads, row_count, HD), jnp.float32),
    )
    running = initial
    key_piece = lax.all_gather(key_rows, "tp", axis=0, tiled=True)
    value_piece = lax.all_gather(value_rows, "tp", axis=0, tiled=True)
    length = key_piece.shape[0]
    step_rows = key_block if length % key_block == 0 else length
    number = length // step_rows
    key_blocks = key_piece.reshape(number, step_rows, local_heads, HD)
    value_blocks = value_piece.reshape(number, step_rows, local_heads, HD)

    def update(carried, blocks_now):
        highest, totals, summed = carried
        key_now, value_now = blocks_now
        scores = (
            jnp.einsum("qhd,khd->hqk", query_heads, key_now, preferred_element_type=jnp.float32)
            * scaling
        )
        new_highest = jnp.maximum(highest, jnp.max(scores, axis=2))
        fading = jnp.exp(highest - new_highest)
        weights = jnp.exp(scores - new_highest[..., None])
        totals = totals * fading + jnp.sum(weights, axis=2)
        summed = summed * fading[..., None] + jnp.einsum(
            "hqk,khd->hqd",
            weights.astype(jnp.bfloat16),
            value_now,
            preferred_element_type=jnp.float32,
        )
        return ((new_highest, totals, summed), None)

    running, unused = lax.scan(update, running, (key_blocks, value_blocks))
    highest, totals, summed = running
    result = summed / totals[..., None]
    return jnp.transpose(result, (1, 0, 2)).reshape(row_count, columns).astype(jnp.bfloat16)


def by_heads_and_rows(projected, hint_gain, block_map, token_perm):
    block_rows = projected.shape[1]
    features = projected.shape[3]
    seq_count = lax.axis_size("seq")
    tp_count = lax.axis_size("tp")
    branch_index = lax.axis_index("branch")
    seq_index = lax.axis_index("seq")
    tp_index = lax.axis_index("tp")
    arrived = lax.all_to_all(projected[0], "seq", split_axis=2, concat_axis=0, tiled=True)
    columns = features // seq_count
    attended = attend(arrived[:, 0], arrived[:, 1], arrived[:, 2])
    attended = lax.optimization_barrier(attended)
    partner = passed_along(attended, "branch", -1)
    perm_table = token_perm.reshape(seq_count, tp_count, block_rows)
    column = lax.dynamic_index_in_dim(perm_table, tp_index, 1, keepdims=False)
    picked = (block_map[:, None] * block_rows + column).reshape(-1)
    control = jnp.take(partner, picked, axis=0).astype(jnp.float32)
    gain_slice = lax.dynamic_slice_in_dim(hint_gain, seq_index * columns, columns)
    summed = (attended.astype(jnp.float32) + gain_slice * control).astype(jnp.bfloat16)
    result = jnp.where(branch_index == 0, summed, attended)
    return lax.all_to_all(result, "seq", split_axis=0, concat_axis=1, tiled=True)[None]


def on_device(projected, hint_gain, block_map, token_perm):
    count = lax.axis_size("seq") * lax.axis_size("tp")
    rows, heads = projected.shape[1], projected.shape[3] // HD
    if heads % count == 0 and count & (count - 1) == 0 and rows % 16 == 0:
        return by_heads(projected, hint_gain, block_map, token_perm)
    return by_heads_and_rows(projected, hint_gain, block_map, token_perm)


def solution(mesh):
    return jax.shard_map(
        on_device,
        mesh=mesh,
        in_specs=(P("branch", ("req", "seq", "tp"), None, None), P(), P(), P()),
        out_specs=P("branch", ("req", "seq", "tp"), None),
        check_vma=False,
    )
```
